128 devices in a mesh: gx: 8 (over z, x_lo), gy: 16 (over x_hi, y, core).
Axes of the slice: x: 4 (x_hi: 2, x_lo: 2; x = x_hi * 2 + x_lo), y: 4, z: 4, core: 2. Of those that a mesh axis runs over, the one named last changes fastest.
Arguments:
- features: bfloat16 [2048, 16, 1024], P(('gx', 'gy')), may hold values from -6 to 6
- brick_position: int32 [2048], P(('gx', 'gy')), may hold values from -1 to 1023, as said below
- brick_count: int32 [128], P(('gx', 'gy')), may hold values from 1 to 16, as said below
- brick_moved: int32 [128], P(('gx', 'gy')), may hold values from 0 to 6, as said below
- weight: bfloat16 [3, 3, 3, 32, 32], replicated, may hold values from -0.21875 to 0.21875
- cotangent: bfloat16 [2048, 16, 1024], P(('gx', 'gy')), may hold values from -6 to 6
Outputs:
- conv_out: bfloat16 [2048, 16, 1024], P(('gx', 'gy'))
- input_grad: bfloat16 [2048, 16, 1024], P(('gx', 'gy'))
- weight_grad: float32 [3, 3, 3, 32, 32], replicated
The draws below stay inside these ranges and needn't reach their ends.
Inputs may be any that keep to these rules, and one draw needn't show every extreme that they name: `brick_count`: slots at and past a device's count are not live. In every draw some device holds 16 live bricks and some device holds 1. A device hands on its last brick_moved live slots; brick_moved[d] <= brick_count[d] and brick_count[d] - brick_moved[d] + brick_moved[p] <= 16 for partner p. In every draw some device hands on 6 bricks. `brick_position`: brick row * 32 + brick column inside the device's tile; distinct among a device's live slots; -1 in slots that are not live.
All inputs are finite; a program needn't handle non-finite values.
Results may differ from the reference program's by a relative error of at most 0.001.
Values may be sent and summed in bfloat16 or wider, within the bound.
A program may use at most 256 MiB of HBM per device.

```python
import math
import jax
import jax.numpy as jnp
from jax import lax

C = 32
FRAMES = 2
BRICK = 16
TILE_BRICK_ROWS = 32
TILE_BRICK_COLS = 32
SLOT_TOTAL = 16
MOVE = 6
HALF_GY = 8
PARTNER_COUNT = 64
SLOTS = 2048
N_GX = 8
N_GY = 16


def brick_plan(key):
    key_list = jax.random.split(key, 4)
    loaded_side = jax.random.randint(key_list[0], (PARTNER_COUNT,), SLOT_TOTAL // 2, SLOT_TOTAL + 1)
    lighter_side = jax.random.randint(key_list[1], (PARTNER_COUNT,), 1, SLOT_TOTAL // 4 + 1)
    chosen = jax.random.randint(key_list[2], (), 0, PARTNER_COUNT)
    flagged = jnp.arange(PARTNER_COUNT) == chosen
    loaded_side = jnp.where(flagged, SLOT_TOTAL, loaded_side)
    lighter_side = jnp.where(flagged, 1, lighter_side)
    heavy_side = jax.random.randint(key_list[3], (PARTNER_COUNT,), 0, 2)
    shipped = jnp.minimum((loaded_side - lighter_side) // 2, MOVE)
    device_numbers = jnp.arange(2 * PARTNER_COUNT)
    column = device_numbers % (2 * HALF_GY)
    pair_ids = device_numbers // (2 * HALF_GY) * HALF_GY + column % HALF_GY
    is_heavy = column // HALF_GY == heavy_side[pair_ids]
    count_table = jnp.where(is_heavy, loaded_side[pair_ids], lighter_side[pair_ids])
    moved = jnp.where(is_heavy, shipped[pair_ids], 0)
    return (count_table.astype(jnp.int32), moved.astype(jnp.int32))


def draw_brick_count(key, part):
    return brick_plan(key)[0]


def draw_brick_moved(key, part):
    return brick_plan(key)[1]


def draw_brick_position(key, part):
    count_table = brick_plan(key)[0]
    key = jax.random.fold_in(key, 7)
    tile_list = jax.random.split(key, 2 * PARTNER_COUNT)
    positions = jax.vmap(lambda tile_lookup_key: jax.random.permutation(tile_lookup_key, TILE_BRICK_ROWS * TILE_BRICK_COLS)[:SLOT_TOTAL])(tile_list)
    occupied = jnp.arange(SLOT_TOTAL)[None, :] < count_table[:, None]
    return jnp.where(occupied, positions, -1).astype(jnp.int32).reshape(-1)


def level_of(key, dims, pieces, smallest, largest):
    factor_of, own = 1.0, jax.random.fold_in(key, 6)
    for axis_at, blocks in pieces:
        heights = jnp.exp(jax.random.uniform(jax.random.fold_in(own, axis_at), (blocks,), jnp.float32, smallest / len(pieces), largest / len(pieces)))
        factor_of = factor_of * jnp.repeat(heights, dims[axis_at] // blocks).reshape([-1 if axis == axis_at else 1 for axis in range(len(dims))])
    return factor_of


def centred(own_key, shape, spread, reach, cuts=(), kind=jnp.bfloat16):
    array = spread * jax.random.normal(own_key, shape, jnp.float32)
    if cuts:
        array = array * level_of(own_key, shape, cuts, -0.22, 0.18)
    return jnp.clip(array, -reach, reach).astype(kind)


def setup_inputs(seed: int = 0) -> dict:
    keys = jax.random.split(jax.random.key(seed), 7)
    return {
        "features": centred(keys[0], (SLOTS, BRICK, BRICK * FRAMES * C), 1.0, 6.0, ((0, 128),)),
        "brick_position": draw_brick_position(jax.random.fold_in(keys[6], 71), 0),
        "brick_count": draw_brick_count(jax.random.fold_in(keys[6], 71), 0),
        "brick_moved": draw_brick_moved(jax.random.fold_in(keys[6], 71), 0),
        "weight": centred(keys[4], (3, 3, 3, C, C), (27 * C) ** -0.5, 0.21875),
        "cotangent": centred(keys[5], (SLOTS, BRICK, BRICK * FRAMES * C), 1.0, 6.0, ((0, 128),)),
    }


def time_blocks(weight, frames):
    channels = weight.shape[3]
    empty = jnp.zeros(weight.shape[:2] + (channels, channels), weight.dtype)
    row_parts = []
    for frame_in in range(frames):
        column_parts = []
        for frame_out in range(frames):
            offset = frame_in - frame_out + 1
            column_parts.append(weight[:, :, offset] if 0 <= offset <= 2 else empty)
        row_parts.append(jnp.concatenate(column_parts, axis=3))
    return jnp.concatenate(row_parts, axis=2)

def fold_time(effective, frames, channels):
    parts = []
    for offset in range(3):
        total = jnp.zeros(effective.shape[:2] + (channels, channels), jnp.float32)
        for frame_in in range(frames):
            for frame_out in range(frames):
                if frame_in - frame_out + 1 == offset:
                    total = total + effective[:, :, frame_in * channels:(frame_in + 1) * channels, frame_out * channels:(frame_out + 1) * channels]
        parts.append(total)
    return jnp.stack(parts, axis=2)

def kernel_tap_sum(padded, block_list, tile_side, time_depth):
    count = padded.shape[0]
    total = jnp.zeros((count * tile_side * tile_side, time_depth), jnp.float32)
    for shift_x in range(3):
        for shift_y in range(3):
            window = padded[:, shift_x:shift_x + tile_side, shift_y:shift_y + tile_side, :].reshape(count * tile_side * tile_side, time_depth)
            total = total + jnp.dot(window, block_list[shift_x, shift_y], preferred_element_type=jnp.float32)
    return total

def tap_grad(padded, gradient_list, tile_side, time_depth):
    count = padded.shape[0]
    flat = gradient_list.reshape(count * tile_side * tile_side, time_depth)
    outer = []
    for shift_x in range(3):
        inner = []
        for shift_y in range(3):
            window = padded[:, shift_x:shift_x + tile_side, shift_y:shift_y + tile_side, :].reshape(count * tile_side * tile_side, time_depth)
            inner.append(jnp.dot(window.T, flat, preferred_element_type=jnp.float32))
        outer.append(jnp.stack(inner))
    return jnp.stack(outer)

def reference(features, brick_position, brick_count, brick_moved, weight, cotangent):
    device_list = N_GX * N_GY
    tile_side = BRICK
    time_depth = FRAMES * C
    ordering = jnp.arange(SLOT_TOTAL, dtype=jnp.int32)
    device_numbers = jnp.arange(device_list, dtype=jnp.int32)
    partner_tile = jnp.bitwise_xor(device_numbers, HALF_GY).astype(jnp.int32)
    retained = brick_count - brick_moved
    retained_partner = retained[partner_tile]
    owned_bricks = device_numbers[:, None] * SLOT_TOTAL + ordering[None, :]
    displaced = partner_tile[:, None] * SLOT_TOTAL + retained_partner[:, None] + ordering[None, :] - retained[:, None]
    displaced = jnp.clip(displaced, 0, SLOTS - 1).astype(jnp.int32)
    source = jnp.where(ordering[None, :] < retained[:, None], owned_bricks, displaced).reshape(-1)
    occupied = ordering[None, :] < brick_count[:, None]
    live_rows = occupied.reshape(-1)[:, None, None]
    gradient_list = jnp.where(live_rows, jnp.take(cotangent, source, axis=0), jnp.zeros_like(cotangent))
    input_list = jnp.where(live_rows, features, jnp.zeros_like(features))
    grid_rows = TILE_BRICK_ROWS * N_GX
    grid_columns = TILE_BRICK_COLS * N_GY
    local_part = jnp.clip(brick_position.reshape(device_list, SLOT_TOTAL), 0, TILE_BRICK_ROWS * TILE_BRICK_COLS - 1)
    row_all = (device_numbers // N_GY)[:, None] * TILE_BRICK_ROWS + local_part // TILE_BRICK_COLS
    column_all = (device_numbers % N_GY)[:, None] * TILE_BRICK_COLS + local_part % TILE_BRICK_COLS
    outside = grid_rows * grid_columns
    flat = jnp.where(occupied, row_all * grid_columns + column_all, outside).reshape(-1)
    slot_map = jnp.full((outside + 1,), SLOTS, jnp.int32).at[flat].set(jnp.arange(SLOTS, dtype=jnp.int32))
    slot_map = slot_map.at[outside].set(SLOTS)

    def neighbour(step_row, step_column):
        row_near = row_all + step_row
        column_near = column_all + step_column
        inside = (row_near >= 0) & (row_near < grid_rows) & (column_near >= 0) & (column_near < grid_columns)
        where_at = jnp.where(inside, row_near * grid_columns + column_near, outside)
        return jnp.where(inside, slot_map[where_at], SLOTS).astype(jnp.int32)
    nearby = jnp.stack([jnp.stack([neighbour(step_row, step_column) for step_column in (-1, 0, 1)], axis=-1) for step_row in (-1, 0, 1)], axis=-2)

    def strips_of(field):
        grid = field.reshape(SLOTS, tile_side, tile_side, time_depth)
        blank = jnp.zeros((1, tile_side, time_depth), field.dtype)
        return tuple((jnp.concatenate([strip, blank], axis=0) for strip in (grid[:, 0], grid[:, tile_side - 1], grid[:, :, 0], grid[:, :, tile_side - 1])))
    strips_x = strips_of(input_list)
    strips_g = strips_of(gradient_list)
    block_list = time_blocks(weight, FRAMES)
    reversed_taps = jnp.swapaxes(block_list[::-1, ::-1], 2, 3)

    def margins(strips, bricks, ids):
        north, south, west, east = strips
        top = jnp.concatenate([south[ids[:, 0, 0]][:, tile_side - 1:], south[ids[:, 0, 1]], south[ids[:, 0, 2]][:, :1]], axis=1)
        bottom = jnp.concatenate([north[ids[:, 2, 0]][:, tile_side - 1:], north[ids[:, 2, 1]], north[ids[:, 2, 2]][:, :1]], axis=1)
        middle = jnp.concatenate([east[ids[:, 1, 0]][:, :, None], bricks, west[ids[:, 1, 2]][:, :, None]], axis=2)
        return jnp.concatenate([top[:, None], middle, bottom[:, None]], axis=1)

    def single_device(bundle):
        ids, bricks_x, bricks_g, alive = bundle
        padded_input = margins(strips_x, bricks_x, ids)
        padded_gradient = margins(strips_g, bricks_g, ids)
        mask = alive[:, None, None]
        output_value = kernel_tap_sum(padded_input, block_list, tile_side, time_depth).astype(jnp.bfloat16).reshape(SLOT_TOTAL, tile_side, tile_side * time_depth)
        returned_value = kernel_tap_sum(padded_gradient, reversed_taps, tile_side, time_depth).astype(jnp.bfloat16).reshape(SLOT_TOTAL, tile_side, tile_side * time_depth)
        partial_value = tap_grad(padded_input, bricks_g, tile_side, time_depth)
        return (jnp.where(mask, output_value, jnp.zeros_like(output_value)), jnp.where(mask, returned_value, jnp.zeros_like(returned_value)), partial_value)
    output_list, returned_values, partial_sums = lax.map(single_device, (nearby, input_list.reshape(device_list, SLOT_TOTAL, tile_side, tile_side, time_depth), gradient_list.reshape(device_list, SLOT_TOTAL, tile_side, tile_side, time_depth), occupied))
    output_list = output_list.reshape(SLOTS, tile_side, tile_side * time_depth)
    landed = (ordering[None, :] < (retained + brick_moved[partner_tile])[:, None]).reshape(-1)[:, None, None]
    conv_out = jnp.where(landed, jnp.take(output_list, source, axis=0), jnp.zeros_like(output_list))
    input_grad = returned_values.reshape(SLOTS, tile_side, tile_side * time_depth)
    scale = 1.0 / math.sqrt(SLOTS * tile_side * tile_side * FRAMES)
    weight_grad = fold_time(lax.optimization_barrier(jnp.sum(partial_sums, axis=0)), FRAMES, C) * scale
    return (conv_out, input_grad, weight_grad)
```

```python
import functools
import math

import jax
import jax.numpy as jnp
from jax import lax
from jax.experimental import pallas as pl
from jax.experimental.pallas import tpu as pltpu
from jax.sharding import PartitionSpec as P

TILE_BRICK_ROWS = 32
TILE_BRICK_COLS = 32
MOVE = 6
SLOTS = 16
SIDE = 16
CELLS = SLOTS * SIDE
WIDTH = 1024
LANES = 128
CAND = 640
CENTRE = 384
ROW_KEY = 1024.0
DEAD = -float(1 << 23)
DEAD_TARGET = -float(1 << 22)
BF = jnp.bfloat16
F32 = jnp.float32
MESH = pl.DeviceIdType.MESH


def dot(a, b):
    return jnp.dot(a, b, preferred_element_type=F32)


def kernel(
    ngx,
    ngy,
    pos_ref,
    count_ref,
    moved_ref,
    x_ref,
    c_ref,
    w_ref,
    conv_ref,
    grad_ref,
    wg_ref,
    lent,
    borrowed,
    lent_y,
    borrowed_y,
    y_ref,
    strips,
    cand_c,
    cand_s,
    key_send,
    key_side,
    key_edge,
    key_corner,
    col_key,
    hot_s,
    hot_c,
    wide,
    band_f,
    band_b,
    part,
    inbox1,
    mine,
    inbox2,
    total,
    key_sems,
    halo_sems,
    lend_sems,
    send1,
    recv1,
    send2,
    recv2,
    send3,
    recv3,
):
    gx = lax.axis_index("gx")
    gy = lax.axis_index("gy")
    half = ngy // 2
    chunk = 256 // ngy
    partner = lax.rem(gy + half, ngy)
    north, south = lax.rem(gx + ngx - 1, ngx), lax.rem(gx + 1, ngx)
    west, east = lax.rem(gy + ngy - 1, ngy), lax.rem(gy + 1, ngy)

    barrier = pltpu.get_barrier_semaphore()
    peers = [(gx, lax.rem(gy + o, ngy)) for o in range(1, ngy)]
    peers += [(lax.rem(gx + o, ngx), gy) for o in range(1, ngx)]
    peers += [(north, west), (north, east), (south, west), (south, east)]
    for peer in peers:
        pl.semaphore_signal(barrier, inc=1, device_id=peer, device_id_type=MESH)

    count = count_ref[0]
    moved = moved_ref[0]
    kept = count - moved

    for j in range(MOVE):
        lent[j] = c_ref[jnp.clip(kept + j, 0, SLOTS - 1)]

    sub = lax.broadcasted_iota(jnp.int32, (SIDE, LANES), 0)
    lane = lax.broadcasted_iota(jnp.int32, (8, CELLS), 1)
    lane_edge = lax.broadcasted_iota(jnp.int32, (8, LANES), 1)
    row_key = jnp.full((8, CELLS), DEAD, F32)
    north_key = jnp.full((8, LANES), DEAD, F32)
    for i in range(SLOTS):
        at = pos_ref[i]
        at = jnp.clip(at, 0, TILE_BRICK_ROWS * TILE_BRICK_COLS - 1)
        brick_row = gx * TILE_BRICK_ROWS + lax.shift_right_logical(at, 5)
        brick_col = gy * TILE_BRICK_COLS + lax.bitwise_and(at, 31)
        key = brick_row * (SIDE * 1024) + brick_col
        live = i < count
        target = jnp.where(live, key, int(DEAD_TARGET))
        source = jnp.where(live, key, int(DEAD))
        col_key[i * SIDE : (i + 1) * SIDE, :] = (sub * 1024 + target).astype(F32)
        wide_key = (jnp.zeros((8, CELLS), jnp.int32) + source).astype(F32)
        row_key = jnp.where(lax.shift_right_logical(lane, 4) == i, wide_key, row_key)
        north_key = jnp.where(
            lax.bitwise_and(lane_edge, 15) == i, wide_key[:, :LANES], north_key
        )
    row_key = row_key + lax.bitwise_and(lane, 15).astype(F32) * ROW_KEY
    south_key = north_key + (SIDE - 1) * ROW_KEY
    dead = jnp.full((8, LANES), DEAD, F32)

    def between(low, value):
        return jnp.where((lane_edge >= low) & (lane_edge < low + 16), value, dead)

    key_send[0] = row_key[:, :LANES]
    key_send[1] = row_key[:, LANES:]
    key_send[2] = between(0, south_key)
    key_send[3] = between(16, north_key)
    key_send[4] = between(32, south_key)
    key_send[5] = between(48, north_key)

    pick_row = lax.broadcasted_iota(jnp.int32, (32, CELLS), 0)
    pick_col = lax.broadcasted_iota(jnp.int32, (32, CELLS), 1)
    picked = lax.bitwise_and(pick_row, 15) * SIDE + lax.shift_right_logical(pick_row, 4) * 15
    pick = jnp.where(pick_col == picked, 1.0, 0.0).astype(BF)
    strips[0] = dot(pick, x_ref[...].reshape(CELLS, WIDTH)).astype(BF)

    pl.semaphore_wait(barrier, len(peers))

    def remote(src, dst, sems, at, peer):
        return pltpu.make_async_remote_copy(
            src_ref=src,
            dst_ref=dst,
            send_sem=sems.at[0, at],
            recv_sem=sems.at[1, at],
            device_id=peer,
            device_id_type=MESH,
        )

    def halo(field, bricks):
        last = pl.ds(WIDTH - LANES, LANES)
        first = pl.ds(0, LANES)
        n_rows, s_rows = pl.ds(0, 16), pl.ds(16, 16)
        edge_n, edge_s = pl.ds(CELLS, 16), pl.ds(CELLS + 16, 16)
        corner_n, corner_s = pl.ds(2 * CELLS + 32, 16), pl.ds(2 * CELLS + 48, 16)
        side = pl.ds(CELLS, CELLS)
        own = bricks
        s = strips.at[field]
        c = cand_c.at[field]
        left, right = cand_s.at[field, 0], cand_s.at[field, 1]
        plan = [
            (own.at[:, first], right.at[side, :], (gx, west)),
            (own.at[:, last], left.at[side, :], (gx, east)),
            (s.at[n_rows, :], c.at[edge_s, :], (north, gy)),
            (s.at[s_rows, :], c.at[edge_n, :], (south, gy)),
            (s.at[n_rows, first], right.at[corner_s, :], (north, west)),
            (s.at[n_rows, last], left.at[corner_s, :], (north, east)),
            (s.at[s_rows, first], right.at[corner_n, :], (south, west)),
            (s.at[s_rows, last], left.at[corner_n, :], (south, east)),
        ]
        return [
            remote(src, dst, halo_sems.at[field], at, peer)
            for at, (src, dst, peer) in enumerate(plan)
        ]

    lend = remote(lent, borrowed, lend_sems.at[0], 0, (gx, partner))
    lend.start()
    cand_c[0, :CELLS, :] = x_ref[...].reshape(CELLS, WIDTH)
    key_plan = [
        (key_send.at[pl.ds(0, 2)], key_side.at[1], (gx, west)),
        (key_send.at[pl.ds(0, 2)], key_side.at[0], (gx, east)),
        (key_send.at[3], key_edge.at[1], (north, gy)),
        (key_send.at[2], key_edge.at[0], (south, gy)),
        (key_send.at[5], key_corner.at[1, 1], (north, west)),
        (key_send.at[5], key_corner.at[0, 1], (north, east)),
        (key_send.at[4], key_corner.at[1, 0], (south, west)),
        (key_send.at[4], key_corner.at[0, 0], (south, east)),
    ]
    keys = [
        remote(src, dst, key_sems, at, peer) for at, (src, dst, peer) in enumerate(key_plan)
    ]
    for copy in keys:
        copy.start()
    x_halo = halo(0, cand_c.at[0, pl.ds(0, CELLS)])
    for copy in x_halo:
        copy.start()

    def strip_of(a, frame_in):
        blocks = []
        for b in (2, 1, 0):
            for frame_out in (0, 1):
                blocks.append(w_ref[a, b, frame_in - frame_out + 1].astype(F32))
        z = jnp.zeros((32, 256), F32)
        return jnp.concatenate([z] + blocks + [z], axis=1)

    for a in range(3):
        for frame_in in range(2):
            strip = strip_of(a, frame_in)
            at = 32 * frame_in
            for q in range(1, 7):
                start = 448 - 64 * q
                band_f[a, 64 * q + at : 64 * q + at + 32, :] = strip[
                    :, start : start + 256
                ].astype(BF)
            for q in (0, 7):
                band_f[a, 64 * q + at : 64 * q + at + 32, :] = jnp.zeros((32, 256), BF)
            for j in range(4):
                start = 192 - 64 * j
                band_b[2 - a, 64 * j + at : 64 * j + at + 32, :] = strip[
                    :, start : start + 512
                ].astype(BF)

    for field in range(2):
        cand_c[field, CELLS + 32 :, :] = jnp.zeros((CENTRE - CELLS - 32, WIDTH), BF)
        for s in range(2):
            cand_s[field, s, 2 * CELLS + 64 :, :] = jnp.zeros((CAND - 2 * CELLS - 64, LANES), BF)

    for copy in keys:
        copy.wait()
    edge_key = jnp.maximum(key_edge[0], key_edge[1])
    for s in range(2):
        corner_key = jnp.maximum(key_corner[s, 0], key_corner[s, 1])
        tail_key = jnp.maximum(edge_key, corner_key)
        keys_at = [key_send[0], key_send[1], key_side[s, 0], key_side[s, 1], tail_key]
        for a in range(3):
            target = col_key[...] + ((a - 1) * ROW_KEY + (2 * s - 1))
            for t, candidate in enumerate(keys_at):
                hot = jnp.where(target == candidate[0:1, :], 1.0, 0.0).astype(BF)
                hot_s[s, a * CELLS : (a + 1) * CELLS, t * LANES : (t + 1) * LANES] = hot
    for at, a in enumerate((0, 2)):
        target = col_key[...] + (a - 1) * ROW_KEY
        for t, candidate in enumerate([key_send[0], key_send[1], edge_key]):
            hot = jnp.where(target == candidate[0:1, :], 1.0, 0.0).astype(BF)
            hot_c[at * CELLS : (at + 1) * CELLS, t * LANES : (t + 1) * LANES] = hot

    def widen(field):
        c = cand_c.at[field]
        for s, (start, to) in enumerate(((WIDTH - LANES, 0), (0, WIDTH + LANES))):
            cs = cand_s.at[field, s]
            cs[:CELLS, :] = c[:CELLS, start : start + LANES]
            cs[2 * CELLS : 2 * CELLS + 32, :] = c[CELLS : CELLS + 32, start : start + LANES]
            found = dot(hot_s[s], cs[...]).astype(BF)
            for a in range(3):
                wide[field, a, :, to : to + LANES] = found[a * CELLS : (a + 1) * CELLS]
        found = dot(hot_c[...], c[...]).astype(BF)
        wide[field, 0, :, LANES : LANES + WIDTH] = found[:CELLS]
        wide[field, 1, :, LANES : LANES + WIDTH] = c[:CELLS, :]
        wide[field, 2, :, LANES : LANES + WIDTH] = found[CELLS:]

    for copy in x_halo:
        copy.wait()
    widen(0)

    lend.wait()
    for i in range(SLOTS):
        guest = borrowed[jnp.clip(i - kept, 0, MOVE - 1)]
        value = lax.select(
            i < kept, c_ref[i], lax.select(i < count, guest, jnp.zeros_like(guest))
        )
        cand_c[1, i * SIDE : (i + 1) * SIDE, :] = value
    strips[1] = dot(pick, cand_c[1, :CELLS, :]).astype(BF)
    g_halo = halo(1, cand_c.at[1, pl.ds(0, CELLS)])
    for copy in g_halo:
        copy.start()

    flipped = cand_c[1, :CELLS, :].T
    low = lax.broadcasted_iota(jnp.int32, (32, LANES), 1)
    keep = low < 64
    blocks = []
    for a in range(3):
        outer = jnp.zeros((256, 512), F32)
        for group in range(4):
            outer = outer + dot(
                flipped[256 * group : 256 * group + 256, :],
                wide[0, a, :, 256 * group : 256 * group + 512],
            )
        for b in range(3):
            sums = [jnp.zeros((64, LANES), F32), jnp.zeros((64, LANES), F32)]
            for j in range(4):
                column = j + b + 1
                tile = column // 2
                sums[column % 2] = (
                    sums[column % 2]
                    + outer[64 * j : 64 * j + 64, LANES * tile : LANES * tile + LANES]
                )
            both = sums[0] + pltpu.roll(sums[1], 64, 1)
            top = jnp.where(keep, both[:32], 0.0)
            bottom = jnp.where(keep, both[32:], 0.0)
            blocks.append(bottom + pltpu.roll(top, 32, 1))
    ninth = blocks[8]
    for s in range(3):
        piece = jnp.where((low >= 32 * s) & (low < 32 * s + 32), ninth, 0.0)
        blocks[s] = blocks[s] + pltpu.roll(piece, 96 - 32 * s, 1)
    for ab in range(8):
        part[32 * ab : 32 * ab + 32, :] = blocks[ab]

    round1 = []
    for o in range(1, ngy):
        to = lax.rem(gy + o, ngy)
        round1.append(
            pltpu.make_async_remote_copy(
                src_ref=part.at[pl.ds(pl.multiple_of(to * chunk, chunk), chunk), :],
                dst_ref=inbox1.at[o],
                send_sem=send1.at[o],
                recv_sem=recv1.at[o],
                device_id=(gx, to),
                device_id_type=MESH,
            )
        )
    for copy in round1:
        copy.start()

    def convolve(field, apply):
        for group in range(4):
            value = jnp.zeros((CELLS, 256), F32)
            for a in range(3):
                value = value + apply(a, wide[field, a, :, 256 * group : 256 * group + 512])
            yield group, value

    slot_row = lax.broadcasted_iota(jnp.int32, (CELLS, 256), 0)
    live_rows = slot_row < count * SIDE
    for group, value in convolve(0, lambda a, rows: dot(rows, band_f[a])):
        value = jnp.where(live_rows, value, 0.0).astype(BF)
        y_ref[:, :, 256 * group : 256 * group + 256] = value.reshape(SLOTS, SIDE, 256)
    for j in range(MOVE):
        brick = y_ref[jnp.clip(kept + j, 0, SLOTS - 1)]
        lent_y[j] = lax.select(j < moved, brick, jnp.zeros_like(brick))
    lend_y = remote(lent_y, borrowed_y, lend_sems.at[1], 0, (gx, partner))
    lend_y.start()

    for copy in round1:
        copy.wait_recv()
    own_rows = part[pl.ds(pl.multiple_of(gy * chunk, chunk), chunk), :]
    for o in range(1, ngy):
        own_rows = own_rows + inbox1[o]
    mine[...] = own_rows
    inbox2[gx] = own_rows
    round2 = []
    for o in range(1, ngx):
        to = lax.rem(gx + o, ngx)
        round2.append(
            pltpu.make_async_remote_copy(
                src_ref=mine,
                dst_ref=inbox2.at[gx],
                send_sem=send2.at[o],
                recv_sem=recv2.at[o],
                device_id=(to, gy),
                device_id_type=MESH,
            )
        )
    for copy in round2:
        copy.start()

    for copy in g_halo:
        copy.wait()
    widen(1)
    by_rows = (((1,), (1,)), ((), ()))
    for group, value in convolve(
        1,
        lambda a, rows: lax.dot_general(rows, band_b[a], by_rows, preferred_element_type=F32),
    ):
        value = jnp.where(live_rows, value, 0.0).astype(BF)
        grad_ref[:, :, 256 * group : 256 * group + 256] = value.reshape(SLOTS, SIDE, 256)

    for copy in round2:
        copy.wait_recv()
    chunk_sum = inbox2[0]
    for o in range(1, ngx):
        chunk_sum = chunk_sum + inbox2[o]
    scale = 1.0 / math.sqrt(SLOTS * ngx * ngy * SIDE * SIDE * 2)
    own_chunk = pl.ds(pl.multiple_of(gy * chunk, chunk), chunk)
    total[own_chunk, :] = chunk_sum * scale
    round3 = []
    for o in range(1, ngy):
        to = lax.rem(gy + o, ngy)
        round3.append(
            pltpu.make_async_remote_copy(
                src_ref=total.at[own_chunk, :],
                dst_ref=total.at[own_chunk, :],
                send_sem=send3.at[o],
                recv_sem=recv3.at[o],
                device_id=(gx, to),
                device_id_type=MESH,
            )
        )
    for copy in round3:
        copy.start()

    lend_y.wait()
    for i in range(SLOTS):
        guest = borrowed_y[jnp.clip(i - kept, 0, MOVE - 1)]
        guest = lax.select(i < kept + MOVE, guest, jnp.zeros_like(guest))
        conv_ref[i] = lax.select(i < kept, y_ref[i], guest)

    for copy in round1:
        copy.wait_send()
    for copy in round2:
        copy.wait_send()
    for copy in round3:
        copy.wait()

    for h in range(2):
        turned = total[128 * h : 128 * h + 128, :].T
        for at in range(4):
            ab = 4 * h + at
            for s in range(3):
                wg_ref[ab // 3, ab % 3, s] = turned[32 * s : 32 * s + 32, 32 * at : 32 * at + 32]
        if h == 0:
            for s in range(3):
                wg_ref[2, 2, s] = turned[96:128, 32 * s : 32 * s + 32]


def local(features, brick_position, brick_count, brick_moved, weight, cotangent):
    ngx, ngy = lax.axis_size("gx"), lax.axis_size("gy")
    chunk = 256 // ngy
    smem = pl.BlockSpec(memory_space=pltpu.SMEM)
    vmem = pl.BlockSpec(memory_space=pltpu.VMEM)
    bricks = (SLOTS, SIDE, WIDTH)
    dma = pltpu.SemaphoreType.DMA
    return pl.pallas_call(
        functools.partial(kernel, ngx, ngy),
        out_shape=(
            jax.ShapeDtypeStruct(bricks, BF),
            jax.ShapeDtypeStruct(bricks, BF),
            jax.ShapeDtypeStruct((3, 3, 3, 32, 32), F32),
        ),
        in_specs=[smem, smem, smem, vmem, vmem, vmem],
        out_specs=(vmem, vmem, vmem),
        scratch_shapes=[
            pltpu.VMEM((MOVE, SIDE, WIDTH), BF),
            pltpu.VMEM((MOVE, SIDE, WIDTH), BF),
            pltpu.VMEM((MOVE, SIDE, WIDTH), BF),
            pltpu.VMEM((MOVE, SIDE, WIDTH), BF),
            pltpu.VMEM(bricks, BF),
            pltpu.VMEM((2, 32, WIDTH), BF),
            pltpu.VMEM((2, CENTRE, WIDTH), BF),
            pltpu.VMEM((2, 2, CAND, LANES), BF),
            pltpu.VMEM((6, 8, LANES), F32),
            pltpu.VMEM((2, 2, 8, LANES), F32),
            pltpu.VMEM((2, 8, LANES), F32),
            pltpu.VMEM((2, 2, 8, LANES), F32),
            pltpu.VMEM((CELLS, LANES), F32),
            pltpu.VMEM((2, 3 * CELLS, CAND), BF),
            pltpu.VMEM((2 * CELLS, CENTRE), BF),
            pltpu.VMEM((2, 3, CELLS, WIDTH + 2 * LANES), BF),
            pltpu.VMEM((3, 512, 256), BF),
            pltpu.VMEM((3, 256, 512), BF),
            pltpu.VMEM((256, LANES), F32),
            pltpu.VMEM((ngy, chunk, LANES), F32),
            pltpu.VMEM((chunk, LANES), F32),
            pltpu.VMEM((ngx, chunk, LANES), F32),
            pltpu.VMEM((256, LANES), F32),
            dma((2, 8)),
            dma((2, 2, 8)),
            dma((2, 2, 1)),
            dma((ngy,)),
            dma((ngy,)),
            dma((ngx,)),
            dma((ngx,)),
            dma((ngy,)),
            dma((ngy,)),
        ],
        compiler_params=pltpu.CompilerParams(
            collective_id=0, has_side_effects=True, vmem_limit_bytes=48 * 1024 * 1024
        ),
    )(brick_position, brick_count, brick_moved, features, cotangent, weight)


def solution(mesh):
    placed = (
        P(("gx", "gy"), None, None),
        P(("gx", "gy")),
        P(("gx", "gy")),
        P(("gx", "gy")),
        P(),
        P(("gx", "gy"), None, None),
    )
    return jax.shard_map(
        local,
        mesh=mesh,
        in_specs=placed,
        out_specs=(P(("gx", "gy"), None, None), P(("gx", "gy"), None, None), P()),
        check_vma=False,
    )
```

```python
import math

import jax
import jax.numpy as jnp
from jax import lax
from jax.experimental import pallas as pl
from jax.experimental.pallas import tpu as pltpu
from jax.sharding import PartitionSpec as P

TILE_BRICK_ROWS = 32
TILE_BRICK_COLS = 32
MOVE = 6
SLOTS = 16
SIDE = 16
CELLS = SLOTS * SIDE
WIDTH = 1024
LANES = 128
CAND = 640
CENTRE = 384
ROW_KEY = 1024.0
DEAD = -float(1 << 23)
DEAD_TARGET = -float(1 << 22)
BF = jnp.bfloat16
F32 = jnp.float32
MESH = pl.DeviceIdType.MESH
N_GX = 8
N_GY = 16
VMEM_BYTES = 65344 * 1024
PIECES = 4
NEAR = 8
FAR = 16
CHUNK = 256 // NEAR
WEST, EAST, NORTH, SOUTH = (0, -1), (0, 1), (-1, 0), (1, 0)
NORTH_WEST, NORTH_EAST, SOUTH_WEST, SOUTH_EAST = (-1, -1), (-1, 1), (1, -1), (1, 1)
STEPS = (WEST, EAST, NORTH, SOUTH, NORTH_WEST, NORTH_EAST, SOUTH_WEST, SOUTH_EAST)


def twice(steps):
    return tuple((2 * row, 2 * col) for row, col in steps)


def dot(a, b):
    return jnp.dot(a, b, preferred_element_type=F32)


def kernel(
    pos_ref,
    count_ref,
    moved_ref,
    x_hbm,
    c_hbm,
    w_hbm,
    conv_hbm,
    grad_hbm,
    sum_hbm,
    conv_ref,
    grad_ref,
    c_ref,
    w_ref,
    lent,
    borrowed,
    lent_y,
    borrowed_y,
    y_ref,
    strips,
    cand_c,
    cand_s,
    key_send,
    key_side,
    key_edge,
    key_corner,
    col_key,
    hot_s,
    hot_c,
    wide,
    band_f,
    band_b,
    part,
    inbox1,
    mine,
    inbox2,
    total,
    in_sems,
    out_sems,
    key_sems,
    halo_sems,
    lend_sems,
    send1,
    recv1,
    send2,
    recv2,
    send3,
    recv3,
    ready,
):
    gx = lax.axis_index("gx")
    gy = lax.axis_index("gy")

    fetches = [
        pltpu.make_async_copy(src, dst, in_sems.at[at])
        for at, (src, dst) in enumerate(
            ((c_hbm, c_ref), (x_hbm, cand_c.at[0, pl.ds(0, CELLS), :]), (w_hbm, w_ref))
        )
    ]
    for fetch in fetches:
        fetch.start()

    def there(step):
        row, col = gx + step[0], gy + step[1]
        return (row >= 0) & (row < N_GX) & (col >= 0) & (col < N_GY)

    def place(step):
        return jnp.clip(gx + step[0], 0, N_GX - 1), jnp.clip(gy + step[1], 0, N_GY - 1)

    def back(step):
        return -step[0], -step[1]

    def how_many(steps):
        return sum(jnp.where(there(step), 1, 0) for step in steps)

    def signal(semaphore, peer):
        pl.semaphore_signal(semaphore, inc=1, device_id=peer, device_id_type=MESH)

    def signal_steps(semaphore, steps):
        for step in steps:

            @pl.when(there(step))
            def _(step=step):
                signal(semaphore, place(step))

    x_lo, z = lax.rem(gx, 2), lax.div(gx, 2)
    x_hi, y, core = lax.div(gy, 8), lax.rem(lax.div(gy, 2), 4), lax.rem(gy, 2)

    def flip(bit, do):
        return 1 - bit if do else bit

    def flip2(value, by):
        low, high = lax.rem(value, 2), lax.div(value, 2)
        return flip(low, by % 2) + 2 * flip(high, by // 2)

    def near(k):
        to = (flip(x_lo, k & 1), flip(x_hi, k >> 1 & 1), flip(core, k >> 2 & 1))
        rank = to[0] + 2 * to[1] + 4 * to[2]
        return (2 * z + to[0], 8 * to[1] + 2 * y + to[2]), rank

    def far(k):
        return (2 * flip2(z, k & 3) + x_lo, 8 * x_hi + 2 * flip2(y, k >> 2) + core)

    my_near = x_lo + 2 * x_hi + 4 * core
    my_far = z + 4 * y
    partner = near(2)[0]

    @pl.when(how_many(STEPS) < len(STEPS))
    def _():
        key_side[...] = jnp.full(key_side.shape, DEAD, F32)
        key_edge[...] = jnp.full(key_edge.shape, DEAD, F32)
        key_corner[...] = jnp.full(key_corner.shape, DEAD, F32)
        for field in range(2):
            cand_c[field, CELLS : CELLS + 32, :] = jnp.zeros((32, WIDTH), BF)
            for s in range(2):
                cand_s[field, s, CELLS : 2 * CELLS + 64, :] = jnp.zeros((CELLS + 64, LANES), BF)

    barrier = pltpu.get_barrier_semaphore()
    far_side = [near(k)[0] for k in (2, 3, 6, 7)]
    for peer in far_side:
        signal(barrier, peer)
    signal_steps(barrier, STEPS)

    count = count_ref[0]
    moved = moved_ref[0]
    kept = count - moved

    fetches[0].wait()
    for j in range(MOVE):
        lent[j] = c_ref[jnp.clip(kept + j, 0, SLOTS - 1)]

    sub = lax.broadcasted_iota(jnp.int32, (SIDE, LANES), 0)
    lane = lax.broadcasted_iota(jnp.int32, (8, CELLS), 1)
    lane_edge = lax.broadcasted_iota(jnp.int32, (8, LANES), 1)
    row_key = jnp.full((8, CELLS), DEAD, F32)
    north_key = jnp.full((8, LANES), DEAD, F32)
    for i in range(SLOTS):
        at = pos_ref[i]
        at = jnp.clip(at, 0, TILE_BRICK_ROWS * TILE_BRICK_COLS - 1)
        brick_row = gx * TILE_BRICK_ROWS + lax.shift_right_logical(at, 5)
        brick_col = gy * TILE_BRICK_COLS + lax.bitwise_and(at, 31)
        key = brick_row * (SIDE * 1024) + brick_col
        live = i < count
        target = jnp.where(live, key, int(DEAD_TARGET))
        source = jnp.where(live, key, int(DEAD))
        col_key[i * SIDE : (i + 1) * SIDE, :] = (sub * 1024 + target).astype(F32)
        wide_key = (jnp.zeros((8, CELLS), jnp.int32) + source).astype(F32)
        row_key = jnp.where(lax.shift_right_logical(lane, 4) == i, wide_key, row_key)
        north_key = jnp.where(
            lax.bitwise_and(lane_edge, 15) == i, wide_key[:, :LANES], north_key
        )
    row_key = row_key + lax.bitwise_and(lane, 15).astype(F32) * ROW_KEY
    south_key = north_key + (SIDE - 1) * ROW_KEY
    dead = jnp.full((8, LANES), DEAD, F32)

    def between(low, value):
        return jnp.where((lane_edge >= low) & (lane_edge < low + 16), value, dead)

    key_send[0] = row_key[:, :LANES]
    key_send[1] = row_key[:, LANES:]
    key_send[2] = between(0, south_key)
    key_send[3] = between(16, north_key)
    key_send[4] = between(32, south_key)
    key_send[5] = between(48, north_key)

    pick_row = lax.broadcasted_iota(jnp.int32, (32, CELLS), 0)
    pick_col = lax.broadcasted_iota(jnp.int32, (32, CELLS), 1)
    picked = lax.bitwise_and(pick_row, 15) * SIDE + lax.shift_right_logical(pick_row, 4) * 15
    pick = jnp.where(pick_col == picked, 1.0, 0.0).astype(BF)
    fetches[1].wait()
    strips[0] = dot(pick, cand_c[0, :CELLS, :]).astype(BF)


    pl.semaphore_wait(barrier, how_many(STEPS) + len(far_side))

    def remote(src, dst, sems, at, peer):
        return pltpu.make_async_remote_copy(
            src_ref=src,
            dst_ref=dst,
            send_sem=sems.at[0, at],
            recv_sem=sems.at[1, at],
            device_id=peer,
            device_id_type=MESH,
        )

    def halo(field, bricks):
        last = pl.ds(WIDTH - LANES, LANES)
        first = pl.ds(0, LANES)
        n_rows, s_rows = pl.ds(0, 16), pl.ds(16, 16)
        edge_n, edge_s = pl.ds(CELLS, 16), pl.ds(CELLS + 16, 16)
        corner_n, corner_s = pl.ds(2 * CELLS + 32, 16), pl.ds(2 * CELLS + 48, 16)
        side = pl.ds(CELLS, CELLS)
        own = bricks
        s = strips.at[field]
        c = cand_c.at[field]
        left, right = cand_s.at[field, 0], cand_s.at[field, 1]
        plan = [
            (own.at[:, first], right.at[side, :], WEST),
            (own.at[:, last], left.at[side, :], EAST),
            (s.at[n_rows, :], c.at[edge_s, :], NORTH),
            (s.at[s_rows, :], c.at[edge_n, :], SOUTH),
            (s.at[n_rows, first], right.at[corner_s, :], NORTH_WEST),
            (s.at[n_rows, last], left.at[corner_s, :], NORTH_EAST),
            (s.at[s_rows, first], right.at[corner_n, :], SOUTH_WEST),
            (s.at[s_rows, last], left.at[corner_n, :], SOUTH_EAST),
        ]
        return [
            (remote(src, dst, halo_sems.at[field], at, place(step)), step)
            for at, (src, dst, step) in enumerate(plan)
        ]

    def start_all(copies):
        for copy, step in copies:

            @pl.when(there(step))
            def _(copy=copy):
                copy.start()

    def wait_all(copies):
        for copy, step in copies:

            @pl.when(there(back(step)))
            def _(copy=copy):
                copy.wait_recv()

            @pl.when(there(step))
            def _(copy=copy):
                copy.wait_send()

    lend = remote(lent, borrowed, lend_sems.at[0], 0, partner)
    lend.start()
    row = pl.ds(0, 1)
    key_plan = [
        (key_send.at[pl.ds(0, 2), row], key_side.at[1, :, row], WEST),
        (key_send.at[pl.ds(0, 2), row], key_side.at[0, :, row], EAST),
        (key_send.at[3, row], key_edge.at[1, row], NORTH),
        (key_send.at[2, row], key_edge.at[0, row], SOUTH),
        (key_send.at[5, row], key_corner.at[1, 1, row], NORTH_WEST),
        (key_send.at[5, row], key_corner.at[0, 1, row], NORTH_EAST),
        (key_send.at[4, row], key_corner.at[1, 0, row], SOUTH_WEST),
        (key_send.at[4, row], key_corner.at[0, 0, row], SOUTH_EAST),
    ]
    keys = [
        (remote(src, dst, key_sems, at, place(step)), step)
        for at, (src, dst, step) in enumerate(key_plan)
    ]
    start_all(keys)
    x_halo = halo(0, cand_c.at[0, pl.ds(0, CELLS)])
    start_all(x_halo)

    def side_hot(s, tiles):
        for a in range(3):
            target = col_key[...] + ((a - 1) * ROW_KEY + (2 * s - 1))
            for t, candidate in tiles:
                hot = jnp.where(target == candidate, 1.0, 0.0).astype(BF)
                hot_s[s, a * CELLS : (a + 1) * CELLS, t * LANES : (t + 1) * LANES] = hot

    def centre_hot(tiles):
        for at, a in enumerate((0, 2)):
            target = col_key[...] + (a - 1) * ROW_KEY
            for t, candidate in tiles:
                hot = jnp.where(target == candidate, 1.0, 0.0).astype(BF)
                hot_c[at * CELLS : (at + 1) * CELLS, t * LANES : (t + 1) * LANES] = hot

    own_tiles = [(0, key_send[0, :1]), (1, key_send[1, :1])]
    for s in range(2):
        side_hot(s, own_tiles)
    centre_hot(own_tiles)

    for field in range(2):
        cand_c[field, CELLS + 32 :, :] = jnp.zeros((CENTRE - CELLS - 32, WIDTH), BF)
        for s in range(2):
            cand_s[field, s, 2 * CELLS + 64 :, :] = jnp.zeros((CAND - 2 * CELLS - 64, LANES), BF)

    fetches[2].wait()
    def strip_of(a, frame_in):
        blocks = []
        for b in (2, 1, 0):
            for frame_out in (0, 1):
                blocks.append(w_ref[a, b, frame_in - frame_out + 1].astype(F32))
        z = jnp.zeros((32, 256), F32)
        return jnp.concatenate([z] + blocks + [z], axis=1)

    for a in range(3):
        for frame_in in range(2):
            strip = strip_of(a, frame_in)
            at = 32 * frame_in
            for q in range(1, 7):
                start = 448 - 64 * q
                band_f[a, 64 * q + at : 64 * q + at + 32, :] = strip[
                    :, start : start + 256
                ].astype(BF)
            for q in (0, 7):
                band_f[a, 64 * q + at : 64 * q + at + 32, :] = jnp.zeros((32, 256), BF)
            for j in range(4):
                start = 192 - 64 * j
                band_b[2 - a, 64 * j + at : 64 * j + at + 32, :] = strip[
                    :, start : start + 512
                ].astype(BF)

    wait_all(keys)
    edge_key = jnp.maximum(key_edge[0, :1], key_edge[1, :1])
    for s in range(2):
        corner_key = jnp.maximum(key_corner[s, 0, :1], key_corner[s, 1, :1])
        tail_key = jnp.maximum(edge_key, corner_key)
        side_hot(s, [(2, key_side[s, 0, :1]), (3, key_side[s, 1, :1]), (4, tail_key)])
    centre_hot([(2, edge_key)])

    def widen(field):
        c = cand_c.at[field]
        for s, (start, to) in enumerate(((WIDTH - LANES, 0), (0, WIDTH + LANES))):
            cs = cand_s.at[field, s]
            cs[:CELLS, :] = c[:CELLS, start : start + LANES]
            cs[2 * CELLS : 2 * CELLS + 32, :] = c[CELLS : CELLS + 32, start : start + LANES]
            found = dot(hot_s[s], cs[...]).astype(BF)
            for a in range(3):
                wide[field, a, :, to : to + LANES] = found[a * CELLS : (a + 1) * CELLS]
        found = dot(hot_c[...], c[...]).astype(BF)
        wide[field, 0, :, LANES : LANES + WIDTH] = found[:CELLS]
        wide[field, 1, :, LANES : LANES + WIDTH] = c[:CELLS, :]
        wide[field, 2, :, LANES : LANES + WIDTH] = found[CELLS:]

    wait_all(x_halo)
    signal_steps(ready.at[0], twice(STEPS))
    widen(0)

    lend.wait()
    for i in range(SLOTS):
        guest = borrowed[jnp.clip(i - kept, 0, MOVE - 1)]
        value = lax.select(
            i < kept, c_ref[i], lax.select(i < count, guest, jnp.zeros_like(guest))
        )
        cand_c[1, i * SIDE : (i + 1) * SIDE, :] = value
    strips[1] = dot(pick, cand_c[1, :CELLS, :]).astype(BF)
    g_halo = halo(1, cand_c.at[1, pl.ds(0, CELLS)])

    flipped = cand_c[1, :CELLS, :].T
    low = lax.broadcasted_iota(jnp.int32, (32, LANES), 1)
    keep = low < 64
    blocks = []
    for a in range(3):
        outer = jnp.zeros((256, 512), F32)
        for group in range(4):
            outer = outer + dot(
                flipped[256 * group : 256 * group + 256, :],
                wide[0, a, :, 256 * group : 256 * group + 512],
            )
        for b in range(3):
            sums = [jnp.zeros((64, LANES), F32), jnp.zeros((64, LANES), F32)]
            for j in range(4):
                column = j + b + 1
                tile = column // 2
                sums[column % 2] = (
                    sums[column % 2]
                    + outer[64 * j : 64 * j + 64, LANES * tile : LANES * tile + LANES]
                )
            both = sums[0] + pltpu.roll(sums[1], 64, 1)
            top = jnp.where(keep, both[:32], 0.0)
            bottom = jnp.where(keep, both[32:], 0.0)
            blocks.append(bottom + pltpu.roll(top, 32, 1))
    ninth = blocks[8]
    for s in range(3):
        piece = jnp.where((low >= 32 * s) & (low < 32 * s + 32), ninth, 0.0)
        blocks[s] = blocks[s] + pltpu.roll(piece, 96 - 32 * s, 1)
    for ab in range(8):
        part[32 * ab : 32 * ab + 32, :] = blocks[ab]

    round1 = []
    for k in range(1, NEAR):
        peer, rank = near(k)
        round1.append(
            pltpu.make_async_remote_copy(
                src_ref=part.at[pl.ds(pl.multiple_of(rank * CHUNK, CHUNK), CHUNK), :],
                dst_ref=inbox1.at[k],
                send_sem=send1.at[k],
                recv_sem=recv1.at[k],
                device_id=peer,
                device_id_type=MESH,
            )
        )
    for copy in round1:
        copy.start()

    start_all(g_halo)

    pl.semaphore_wait(ready.at[0], how_many(twice(STEPS)))
    signal_steps(ready.at[1], twice(twice(STEPS)))

    def convolve(field, apply):
        for group in range(4):
            value = jnp.zeros((CELLS, 256), F32)
            for a in range(3):
                value = value + apply(a, wide[field, a, :, 256 * group : 256 * group + 512])
            yield group, value

    slot_row = lax.broadcasted_iota(jnp.int32, (CELLS, 256), 0)
    live_rows = slot_row < count * SIDE
    for group, value in convolve(0, lambda a, rows: dot(rows, band_f[a])):
        value = jnp.where(live_rows, value, 0.0).astype(BF)
        y_ref[:, :, 256 * group : 256 * group + 256] = value.reshape(SLOTS, SIDE, 256)
    for j in range(MOVE):
        brick = y_ref[jnp.clip(kept + j, 0, SLOTS - 1)]
        lent_y[j] = lax.select(j < moved, brick, jnp.zeros_like(brick))
    lend_y = remote(lent_y, borrowed_y, lend_sems.at[1], 0, partner)

    for copy in round1:
        copy.wait_recv()
    own_chunk = pl.ds(pl.multiple_of(my_near * CHUNK, CHUNK), CHUNK)
    own_rows = part[own_chunk, :]
    for k in range(1, NEAR):
        own_rows = own_rows + inbox1[k]
    mine[...] = own_rows
    inbox2[my_far] = own_rows
    pl.semaphore_wait(ready.at[1], how_many(twice(twice(STEPS))))
    round2 = []
    for k in range(1, FAR):
        round2.append(
            pltpu.make_async_remote_copy(
                src_ref=mine,
                dst_ref=inbox2.at[my_far],
                send_sem=send2.at[k],
                recv_sem=recv2.at[k],
                device_id=far(k),
                device_id_type=MESH,
            )
        )
    for copy in round2:
        copy.start()

    lend_y.start()

    wait_all(g_halo)
    widen(1)
    by_rows = (((1,), (1,)), ((), ()))
    for group, value in convolve(
        1,
        lambda a, rows: lax.dot_general(rows, band_b[a], by_rows, preferred_element_type=F32),
    ):
        value = jnp.where(live_rows, value, 0.0).astype(BF)
        grad_ref[:, :, 256 * group : 256 * group + 256] = value.reshape(SLOTS, SIDE, 256)

    grad_out = pltpu.make_async_copy(grad_ref, grad_hbm, out_sems.at[0])
    grad_out.start()

    lend_y.wait()
    for i in range(SLOTS):
        guest = borrowed_y[jnp.clip(i - kept, 0, MOVE - 1)]
        guest = lax.select(i < kept + MOVE, guest, jnp.zeros_like(guest))
        conv_ref[i] = lax.select(i < kept, y_ref[i], guest)

    conv_out = pltpu.make_async_copy(conv_ref, conv_hbm, out_sems.at[1])
    conv_out.start()

    for copy in round2:
        copy.wait_recv()
    chunk_sum = inbox2[0]
    for k in range(1, FAR):
        chunk_sum = chunk_sum + inbox2[k]
    total[own_chunk, :] = chunk_sum * (1.0 / math.sqrt(N_GX * N_GY * SLOTS * SIDE * SIDE * 2))
    round3 = []
    for k in range(1, NEAR):
        round3.append(
            pltpu.make_async_remote_copy(
                src_ref=total.at[own_chunk, :],
                dst_ref=total.at[own_chunk, :],
                send_sem=send3.at[k],
                recv_sem=recv3.at[k],
                device_id=near(k)[0],
                device_id_type=MESH,
            )
        )
    for copy in round3:
        copy.start()
    for copy in round1:
        copy.wait_send()
    for copy in round2:
        copy.wait_send()
    conv_out.wait()
    grad_out.wait()
    for copy in round3:
        copy.wait()
    sum_out = pltpu.make_async_copy(total, sum_hbm, out_sems.at[2])
    sum_out.start()
    sum_out.wait()


def finish(
    conv_in,
    grad_in,
    sum_in,
    conv_hbm,
    grad_hbm,
    wg_hbm,
    stage,
    sum_ref,
    wg_ref,
    in_sems,
    out_sems,
    wg_sems,
):
    sum_copy = pltpu.make_async_copy(sum_in, sum_ref, wg_sems.at[0])
    sum_copy.start()
    fetches, stores = [], []
    for at, (src, dst) in enumerate(((grad_in, grad_hbm), (conv_in, conv_hbm))):
        for part in range(PIECES):
            bricks = pl.ds(part * (SLOTS // PIECES), SLOTS // PIECES)
            held = stage.at[at, bricks]
            fetches.append(pltpu.make_async_copy(src.at[bricks], held, in_sems.at[at, part]))
            stores.append(pltpu.make_async_copy(held, dst.at[bricks], out_sems.at[at, part]))
    for fetch in fetches:
        fetch.start()
    sum_copy.wait()
    for h in range(2):
        turned = sum_ref[128 * h : 128 * h + 128, :].T
        for at in range(4):
            ab = 4 * h + at
            for s in range(3):
                wg_ref[ab // 3, ab % 3, s] = turned[32 * s : 32 * s + 32, 32 * at : 32 * at + 32]
        if h == 0:
            for s in range(3):
                wg_ref[2, 2, s] = turned[96:128, 32 * s : 32 * s + 32]
    wg_copy = pltpu.make_async_copy(wg_ref, wg_hbm, wg_sems.at[1])
    wg_copy.start()
    for fetch, store in zip(fetches, stores):
        fetch.wait()
        store.start()
    for store in stores:
        store.wait()
    wg_copy.wait()


def local(features, brick_position, brick_count, brick_moved, weight, cotangent):
    smem = pl.BlockSpec(memory_space=pltpu.SMEM)
    vmem = pl.BlockSpec(memory_space=pltpu.VMEM)
    hbm = pl.BlockSpec(memory_space=pltpu.HBM)
    bricks = (SLOTS, SIDE, WIDTH)
    taps = (3, 3, 3, 32, 32)
    dma = pltpu.SemaphoreType.DMA
    conv, grad, summed = pl.pallas_call(
        kernel,
        out_shape=(
            jax.ShapeDtypeStruct(bricks, BF),
            jax.ShapeDtypeStruct(bricks, BF),
            jax.ShapeDtypeStruct((256, LANES), F32),
        ),
        in_specs=[smem, smem, smem, hbm, hbm, hbm],
        out_specs=(hbm, hbm, hbm),
        scratch_shapes=[
            pltpu.VMEM(bricks, BF),
            pltpu.VMEM(bricks, BF),
            pltpu.VMEM(bricks, BF),
            pltpu.VMEM(taps, BF),
            pltpu.VMEM((MOVE, SIDE, WIDTH), BF),
            pltpu.VMEM((MOVE, SIDE, WIDTH), BF),
            pltpu.VMEM((MOVE, SIDE, WIDTH), BF),
            pltpu.VMEM((MOVE, SIDE, WIDTH), BF),
            pltpu.VMEM(bricks, BF),
            pltpu.VMEM((2, 32, WIDTH), BF),
            pltpu.VMEM((2, CENTRE, WIDTH), BF),
            pltpu.VMEM((2, 2, CAND, LANES), BF),
            pltpu.VMEM((6, 8, LANES), F32),
            pltpu.VMEM((2, 2, 8, LANES), F32),
            pltpu.VMEM((2, 8, LANES), F32),
            pltpu.VMEM((2, 2, 8, LANES), F32),
            pltpu.VMEM((CELLS, LANES), F32),
            pltpu.VMEM((2, 3 * CELLS, CAND), BF),
            pltpu.VMEM((2 * CELLS, CENTRE), BF),
            pltpu.VMEM((2, 3, CELLS, WIDTH + 2 * LANES), BF),
            pltpu.VMEM((3, 512, 256), BF),
            pltpu.VMEM((3, 256, 512), BF),
            pltpu.VMEM((256, LANES), F32),
            pltpu.VMEM((NEAR, CHUNK, LANES), F32),
            pltpu.VMEM((CHUNK, LANES), F32),
            pltpu.VMEM((FAR, CHUNK, LANES), F32),
            pltpu.VMEM((256, LANES), F32),
            dma((3,)),
            dma((3,)),
            dma((2, 8)),
            dma((2, 2, 8)),
            dma((2, 2, 1)),
            dma((NEAR,)),
            dma((NEAR,)),
            dma((FAR,)),
            dma((FAR,)),
            dma((NEAR,)),
            dma((NEAR,)),
            pltpu.SemaphoreType.REGULAR((2,)),
        ],
        compiler_params=pltpu.CompilerParams(
            collective_id=0, has_side_effects=True, vmem_limit_bytes=VMEM_BYTES
        ),
    )(
        brick_position,
        brick_count,
        brick_moved,
        features.reshape(CELLS, WIDTH),
        cotangent,
        weight,
    )
    return pl.pallas_call(
        finish,
        out_shape=(
            jax.ShapeDtypeStruct(bricks, BF),
            jax.ShapeDtypeStruct(bricks, BF),
            jax.ShapeDtypeStruct(taps, F32),
        ),
        in_specs=[hbm, hbm, hbm],
        out_specs=(hbm, hbm, hbm),
        scratch_shapes=[
            pltpu.VMEM((2,) + bricks, BF),
            pltpu.VMEM((256, LANES), F32),
            pltpu.VMEM(taps, F32),
            dma((2, PIECES)),
            dma((2, PIECES)),
            dma((2,)),
        ],
        compiler_params=pltpu.CompilerParams(vmem_limit_bytes=VMEM_BYTES),
    )(conv, grad, summed)


def solution(mesh):
    placed = (
        P(("gx", "gy"), None, None),
        P(("gx", "gy")),
        P(("gx", "gy")),
        P(("gx", "gy")),
        P(),
        P(("gx", "gy"), None, None),
    )
    return jax.shard_map(
        local,
        mesh=mesh,
        in_specs=placed,
        out_specs=(P(("gx", "gy"), None, None), P(("gx", "gy"), None, None), P()),
        check_vma=False,
    )
```

```python
import math

import jax
import jax.numpy as jnp
from jax import lax
from jax.experimental import pallas as pl
from jax.experimental.pallas import tpu as pltpu
from jax.sharding import PartitionSpec as P

TILE_BRICK_ROWS = 32
TILE_BRICK_COLS = 32
MOVE = 6
SLOTS = 16
SIDE = 16
CELLS = SLOTS * SIDE
WIDTH = 1024
LANES = 128
CAND = 640
CENTRE = 384
ROW_KEY = 1024.0
DEAD = -float(1 << 23)
DEAD_TARGET = -float(1 << 22)
BF = jnp.bfloat16
F32 = jnp.float32
MESH = pl.DeviceIdType.MESH
N_GX = 8
N_GY = 16
VMEM_BYTES = 49152 * 1024
NEAR = 8
FAR = 16
CHUNK = 256 // NEAR
WEST, EAST, NORTH, SOUTH = (0, -1), (0, 1), (-1, 0), (1, 0)
NORTH_WEST, NORTH_EAST, SOUTH_WEST, SOUTH_EAST = (-1, -1), (-1, 1), (1, -1), (1, 1)
STEPS = (WEST, EAST, NORTH, SOUTH, NORTH_WEST, NORTH_EAST, SOUTH_WEST, SOUTH_EAST)


def twice(steps):
    return tuple((2 * row, 2 * col) for row, col in steps)


def dot(a, b):
    return jnp.dot(a, b, preferred_element_type=F32)


def kernel(
    pos_hbm,
    count_ref,
    moved_ref,
    x_hbm,
    c_hbm,
    w_hbm,
    conv_ref,
    grad_ref,
    sum_ref,
    pos_ref,
    c_ref,
    w_ref,
    lent,
    borrowed,
    lent_y,
    borrowed_y,
    y_ref,
    strips,
    cand_c,
    cand_s,
    key_send,
    key_side,
    key_edge,
    key_corner,
    col_key,
    hot_s,
    hot_c,
    wide,
    band_f,
    band_b,
    part,
    inbox1,
    mine,
    inbox2,
    total,
    in_sems,
    key_sems,
    halo_sems,
    lend_sems,
    send1,
    recv1,
    send2,
    recv2,
    send3,
    recv3,
    ready,
):
    gx = lax.axis_index("gx")
    gy = lax.axis_index("gy")

    fetches = [
        pltpu.make_async_copy(src, dst, in_sems.at[at])
        for at, (src, dst) in enumerate(
            (
                (c_hbm, c_ref),
                (x_hbm, cand_c.at[0, pl.ds(0, CELLS), :]),
                (w_hbm, w_ref),
                (pos_hbm, pos_ref),
            )
        )
    ]
    for at in (3, 0, 1, 2):
        fetches[at].start()

    def there(step):
        row, col = gx + step[0], gy + step[1]
        return (row >= 0) & (row < N_GX) & (col >= 0) & (col < N_GY)

    def place(step):
        return jnp.clip(gx + step[0], 0, N_GX - 1), jnp.clip(gy + step[1], 0, N_GY - 1)

    def back(step):
        return -step[0], -step[1]

    def how_many(steps):
        return sum(jnp.where(there(step), 1, 0) for step in steps)

    def signal(semaphore, peer):
        pl.semaphore_signal(semaphore, inc=1, device_id=peer, device_id_type=MESH)

    def signal_steps(semaphore, steps):
        for step in steps:

            @pl.when(there(step))
            def _(step=step):
                signal(semaphore, place(step))

    x_lo, z = lax.rem(gx, 2), lax.div(gx, 2)
    x_hi, y, core = lax.div(gy, 8), lax.rem(lax.div(gy, 2), 4), lax.rem(gy, 2)

    def flip(bit, do):
        return 1 - bit if do else bit

    def flip2(value, by):
        low, high = lax.rem(value, 2), lax.div(value, 2)
        return flip(low, by % 2) + 2 * flip(high, by // 2)

    def near(k):
        to = (flip(x_lo, k & 1), flip(x_hi, k >> 1 & 1), flip(core, k >> 2 & 1))
        rank = to[0] + 2 * to[1] + 4 * to[2]
        return (2 * z + to[0], 8 * to[1] + 2 * y + to[2]), rank

    def far(k):
        return (2 * flip2(z, k & 3) + x_lo, 8 * x_hi + 2 * flip2(y, k >> 2) + core)

    my_near = x_lo + 2 * x_hi + 4 * core
    my_far = z + 4 * y
    partner = near(2)[0]

    @pl.when(how_many(STEPS) < len(STEPS))
    def _():
        key_side[...] = jnp.full(key_side.shape, DEAD, F32)
        key_edge[...] = jnp.full(key_edge.shape, DEAD, F32)
        key_corner[...] = jnp.full(key_corner.shape, DEAD, F32)
        for field in range(2):
            cand_c[field, CELLS : CELLS + 32, :] = jnp.zeros((32, WIDTH), BF)
            for s in range(2):
                cand_s[field, s, CELLS : 2 * CELLS + 64, :] = jnp.zeros((CELLS + 64, LANES), BF)

    barrier = pltpu.get_barrier_semaphore()
    far_side = [near(k)[0] for k in (2, 3, 6, 7)]
    for peer in far_side:
        signal(barrier, peer)
    signal_steps(barrier, STEPS)

    fetches[3].wait()
    count = count_ref[0]
    moved = moved_ref[0]
    kept = count - moved

    fetches[0].wait()
    for j in range(MOVE):
        lent[j] = c_ref[jnp.clip(kept + j, 0, SLOTS - 1)]

    sub = lax.broadcasted_iota(jnp.int32, (SIDE, LANES), 0)
    lane = lax.broadcasted_iota(jnp.int32, (8, CELLS), 1)
    lane_edge = lax.broadcasted_iota(jnp.int32, (8, LANES), 1)
    row_key = jnp.full((8, CELLS), DEAD, F32)
    north_key = jnp.full((8, LANES), DEAD, F32)
    for i in range(SLOTS):
        at = pos_ref[i]
        at = jnp.clip(at, 0, TILE_BRICK_ROWS * TILE_BRICK_COLS - 1)
        brick_row = gx * TILE_BRICK_ROWS + lax.shift_right_logical(at, 5)
        brick_col = gy * TILE_BRICK_COLS + lax.bitwise_and(at, 31)
        key = brick_row * (SIDE * 1024) + brick_col
        live = i < count
        target = jnp.where(live, key, int(DEAD_TARGET))
        source = jnp.where(live, key, int(DEAD))
        col_key[i * SIDE : (i + 1) * SIDE, :] = (sub * 1024 + target).astype(F32)
        wide_key = (jnp.zeros((8, CELLS), jnp.int32) + source).astype(F32)
        row_key = jnp.where(lax.shift_right_logical(lane, 4) == i, wide_key, row_key)
        north_key = jnp.where(
            lax.bitwise_and(lane_edge, 15) == i, wide_key[:, :LANES], north_key
        )
    row_key = row_key + lax.bitwise_and(lane, 15).astype(F32) * ROW_KEY
    south_key = north_key + (SIDE - 1) * ROW_KEY
    dead = jnp.full((8, LANES), DEAD, F32)

    def between(low, value):
        return jnp.where((lane_edge >= low) & (lane_edge < low + 16), value, dead)

    key_send[0] = row_key[:, :LANES]
    key_send[1] = row_key[:, LANES:]
    key_send[2] = between(0, south_key)
    key_send[3] = between(16, north_key)
    key_send[4] = between(32, south_key)
    key_send[5] = between(48, north_key)

    pick_row = lax.broadcasted_iota(jnp.int32, (32, CELLS), 0)
    pick_col = lax.broadcasted_iota(jnp.int32, (32, CELLS), 1)
    picked = lax.bitwise_and(pick_row, 15) * SIDE + lax.shift_right_logical(pick_row, 4) * 15
    pick = jnp.where(pick_col == picked, 1.0, 0.0).astype(BF)
    fetches[1].wait()
    strips[0] = dot(pick, cand_c[0, :CELLS, :]).astype(BF)


    pl.semaphore_wait(barrier, how_many(STEPS) + len(far_side))

    def remote(src, dst, sems, at, peer):
        return pltpu.make_async_remote_copy(
            src_ref=src,
            dst_ref=dst,
            send_sem=sems.at[0, at],
            recv_sem=sems.at[1, at],
            device_id=peer,
            device_id_type=MESH,
        )

    def halo(field, bricks):
        last = pl.ds(WIDTH - LANES, LANES)
        first = pl.ds(0, LANES)
        n_rows, s_rows = pl.ds(0, 16), pl.ds(16, 16)
        edge_n, edge_s = pl.ds(CELLS, 16), pl.ds(CELLS + 16, 16)
        corner_n, corner_s = pl.ds(2 * CELLS + 32, 16), pl.ds(2 * CELLS + 48, 16)
        side = pl.ds(CELLS, CELLS)
        own = bricks
        s = strips.at[field]
        c = cand_c.at[field]
        left, right = cand_s.at[field, 0], cand_s.at[field, 1]
        plan = [
            (own.at[:, first], right.at[side, :], WEST),
            (own.at[:, last], left.at[side, :], EAST),
            (s.at[n_rows, :], c.at[edge_s, :], NORTH),
            (s.at[s_rows, :], c.at[edge_n, :], SOUTH),
            (s.at[n_rows, first], right.at[corner_s, :], NORTH_WEST),
            (s.at[n_rows, last], left.at[corner_s, :], NORTH_EAST),
            (s.at[s_rows, first], right.at[corner_n, :], SOUTH_WEST),
            (s.at[s_rows, last], left.at[corner_n, :], SOUTH_EAST),
        ]
        return [
            (remote(src, dst, halo_sems.at[field], at, place(step)), step)
            for at, (src, dst, step) in enumerate(plan)
        ]

    def start_all(copies):
        for copy, step in copies:

            @pl.when(there(step))
            def _(copy=copy):
                copy.start()

    def wait_all(copies):
        for copy, step in copies:

            @pl.when(there(back(step)))
            def _(copy=copy):
                copy.wait_recv()

            @pl.when(there(step))
            def _(copy=copy):
                copy.wait_send()

    lend = remote(lent, borrowed, lend_sems.at[0], 0, partner)
    lend.start()
    row = pl.ds(0, 1)
    key_plan = [
        (key_send.at[pl.ds(0, 2), row], key_side.at[1, :, row], WEST),
        (key_send.at[pl.ds(0, 2), row], key_side.at[0, :, row], EAST),
        (key_send.at[3, row], key_edge.at[1, row], NORTH),
        (key_send.at[2, row], key_edge.at[0, row], SOUTH),
        (key_send.at[5, row], key_corner.at[1, 1, row], NORTH_WEST),
        (key_send.at[5, row], key_corner.at[0, 1, row], NORTH_EAST),
        (key_send.at[4, row], key_corner.at[1, 0, row], SOUTH_WEST),
        (key_send.at[4, row], key_corner.at[0, 0, row], SOUTH_EAST),
    ]
    keys = [
        (remote(src, dst, key_sems, at, place(step)), step)
        for at, (src, dst, step) in enumerate(key_plan)
    ]
    start_all(keys)
    x_halo = halo(0, cand_c.at[0, pl.ds(0, CELLS)])
    start_all(x_halo)

    def side_hot(s, tiles):
        for a in range(3):
            target = col_key[...] + ((a - 1) * ROW_KEY + (2 * s - 1))
            for t, candidate in tiles:
                hot = jnp.where(target == candidate, 1.0, 0.0).astype(BF)
                hot_s[s, a * CELLS : (a + 1) * CELLS, t * LANES : (t + 1) * LANES] = hot

    def centre_hot(tiles):
        for at, a in enumerate((0, 2)):
            target = col_key[...] + (a - 1) * ROW_KEY
            for t, candidate in tiles:
                hot = jnp.where(target == candidate, 1.0, 0.0).astype(BF)
                hot_c[at * CELLS : (at + 1) * CELLS, t * LANES : (t + 1) * LANES] = hot

    own_tiles = [(0, key_send[0, :1]), (1, key_send[1, :1])]
    for s in range(2):
        side_hot(s, own_tiles)
    centre_hot(own_tiles)

    for field in range(2):
        cand_c[field, CELLS + 32 :, :] = jnp.zeros((CENTRE - CELLS - 32, WIDTH), BF)
        for s in range(2):
            cand_s[field, s, 2 * CELLS + 64 :, :] = jnp.zeros((CAND - 2 * CELLS - 64, LANES), BF)

    fetches[2].wait()
    def strip_of(a, frame_in):
        blocks = []
        for b in (2, 1, 0):
            for frame_out in (0, 1):
                blocks.append(w_ref[a, b, frame_in - frame_out + 1].astype(F32))
        z = jnp.zeros((32, 256), F32)
        return jnp.concatenate([z] + blocks + [z], axis=1)

    for a in range(3):
        for frame_in in range(2):
            strip = strip_of(a, frame_in)
            at = 32 * frame_in
            for q in range(1, 7):
                start = 448 - 64 * q
                band_f[a, 64 * q + at : 64 * q + at + 32, :] = strip[
                    :, start : start + 256
                ].astype(BF)
            for q in (0, 7):
                band_f[a, 64 * q + at : 64 * q + at + 32, :] = jnp.zeros((32, 256), BF)
            for j in range(4):
                start = 192 - 64 * j
                band_b[2 - a, 64 * j + at : 64 * j + at + 32, :] = strip[
                    :, start : start + 512
                ].astype(BF)

    wait_all(keys)
    edge_key = jnp.maximum(key_edge[0, :1], key_edge[1, :1])
    for s in range(2):
        corner_key = jnp.maximum(key_corner[s, 0, :1], key_corner[s, 1, :1])
        tail_key = jnp.maximum(edge_key, corner_key)
        side_hot(s, [(2, key_side[s, 0, :1]), (3, key_side[s, 1, :1]), (4, tail_key)])
    centre_hot([(2, edge_key)])

    def widen(field):
        c = cand_c.at[field]
        for s, (start, to) in enumerate(((WIDTH - LANES, 0), (0, WIDTH + LANES))):
            cs = cand_s.at[field, s]
            cs[:CELLS, :] = c[:CELLS, start : start + LANES]
            cs[2 * CELLS : 2 * CELLS + 32, :] = c[CELLS : CELLS + 32, start : start + LANES]
            found = dot(hot_s[s], cs[...]).astype(BF)
            for a in range(3):
                wide[field, a, :, to : to + LANES] = found[a * CELLS : (a + 1) * CELLS]
        found = dot(hot_c[...], c[...]).astype(BF)
        wide[field, 0, :, LANES : LANES + WIDTH] = found[:CELLS]
        wide[field, 1, :, LANES : LANES + WIDTH] = c[:CELLS, :]
        wide[field, 2, :, LANES : LANES + WIDTH] = found[CELLS:]

    wait_all(x_halo)
    signal_steps(ready.at[0], twice(STEPS))
    widen(0)

    lend.wait()
    for i in range(SLOTS):
        guest = borrowed[jnp.clip(i - kept, 0, MOVE - 1)]
        value = lax.select(
            i < kept, c_ref[i], lax.select(i < count, guest, jnp.zeros_like(guest))
        )
        cand_c[1, i * SIDE : (i + 1) * SIDE, :] = value
    strips[1] = dot(pick, cand_c[1, :CELLS, :]).astype(BF)
    g_halo = halo(1, cand_c.at[1, pl.ds(0, CELLS)])

    flipped = cand_c[1, :CELLS, :].T
    low = lax.broadcasted_iota(jnp.int32, (32, LANES), 1)
    keep = low < 64
    blocks = []
    for a in range(3):
        outer = jnp.zeros((256, 512), F32)
        for group in range(4):
            outer = outer + dot(
                flipped[256 * group : 256 * group + 256, :],
                wide[0, a, :, 256 * group : 256 * group + 512],
            )
        for b in range(3):
            sums = [jnp.zeros((64, LANES), F32), jnp.zeros((64, LANES), F32)]
            for j in range(4):
                column = j + b + 1
                tile = column // 2
                sums[column % 2] = (
                    sums[column % 2]
                    + outer[64 * j : 64 * j + 64, LANES * tile : LANES * tile + LANES]
                )
            both = sums[0] + pltpu.roll(sums[1], 64, 1)
            top = jnp.where(keep, both[:32], 0.0)
            bottom = jnp.where(keep, both[32:], 0.0)
            blocks.append(bottom + pltpu.roll(top, 32, 1))
    ninth = blocks[8]
    for s in range(3):
        piece = jnp.where((low >= 32 * s) & (low < 32 * s + 32), ninth, 0.0)
        blocks[s] = blocks[s] + pltpu.roll(piece, 96 - 32 * s, 1)
    for ab in range(8):
        part[32 * ab : 32 * ab + 32, :] = blocks[ab]

    round1 = []
    for k in range(1, NEAR):
        peer, rank = near(k)
        round1.append(
            pltpu.make_async_remote_copy(
                src_ref=part.at[pl.ds(pl.multiple_of(rank * CHUNK, CHUNK), CHUNK), :],
                dst_ref=inbox1.at[k],
                send_sem=send1.at[k],
                recv_sem=recv1.at[k],
                device_id=peer,
                device_id_type=MESH,
            )
        )
    for copy in round1:
        copy.start()

    start_all(g_halo)

    pl.semaphore_wait(ready.at[0], how_many(twice(STEPS)))
    signal_steps(ready.at[1], twice(twice(STEPS)))

    def convolve(field, apply):
        for group in range(4):
            value = jnp.zeros((CELLS, 256), F32)
            for a in range(3):
                value = value + apply(a, wide[field, a, :, 256 * group : 256 * group + 512])
            yield group, value

    slot_row = lax.broadcasted_iota(jnp.int32, (CELLS, 256), 0)
    live_rows = slot_row < count * SIDE
    for group, value in convolve(0, lambda a, rows: dot(rows, band_f[a])):
        value = jnp.where(live_rows, value, 0.0).astype(BF)
        y_ref[:, :, 256 * group : 256 * group + 256] = value.reshape(SLOTS, SIDE, 256)
    for j in range(MOVE):
        brick = y_ref[jnp.clip(kept + j, 0, SLOTS - 1)]
        lent_y[j] = lax.select(j < moved, brick, jnp.zeros_like(brick))
    lend_y = remote(lent_y, borrowed_y, lend_sems.at[1], 0, partner)

    for copy in round1:
        copy.wait_recv()
    own_chunk = pl.ds(pl.multiple_of(my_near * CHUNK, CHUNK), CHUNK)
    own_rows = part[own_chunk, :]
    for k in range(1, NEAR):
        own_rows = own_rows + inbox1[k]
    mine[...] = own_rows
    inbox2[my_far] = own_rows
    pl.semaphore_wait(ready.at[1], how_many(twice(twice(STEPS))))
    round2 = []
    for k in range(1, FAR):
        round2.append(
            pltpu.make_async_remote_copy(
                src_ref=mine,
                dst_ref=inbox2.at[my_far],
                send_sem=send2.at[k],
                recv_sem=recv2.at[k],
                device_id=far(k),
                device_id_type=MESH,
            )
        )
    for copy in round2:
        copy.start()

    lend_y.start()

    wait_all(g_halo)
    widen(1)
    by_rows = (((1,), (1,)), ((), ()))
    for group, value in convolve(
        1,
        lambda a, rows: lax.dot_general(rows, band_b[a], by_rows, preferred_element_type=F32),
    ):
        value = jnp.where(live_rows, value, 0.0).astype(BF)
        grad_ref[:, :, 256 * group : 256 * group + 256] = value.reshape(SLOTS, SIDE, 256)

    lend_y.wait()
    for i in range(SLOTS):
        guest = borrowed_y[jnp.clip(i - kept, 0, MOVE - 1)]
        guest = lax.select(i < kept + MOVE, guest, jnp.zeros_like(guest))
        conv_ref[i] = lax.select(i < kept, y_ref[i], guest)

    for copy in round2:
        copy.wait_recv()
    chunk_sum = inbox2[0]
    for k in range(1, FAR):
        chunk_sum = chunk_sum + inbox2[k]
    total[own_chunk, :] = chunk_sum * (1.0 / math.sqrt(N_GX * N_GY * SLOTS * SIDE * SIDE * 2))
    round3 = []
    for k in range(1, NEAR):
        round3.append(
            pltpu.make_async_remote_copy(
                src_ref=total.at[own_chunk, :],
                dst_ref=total.at[own_chunk, :],
                send_sem=send3.at[k],
                recv_sem=recv3.at[k],
                device_id=near(k)[0],
                device_id_type=MESH,
            )
        )
    for copy in round3:
        copy.start()
    for copy in round1:
        copy.wait_send()
    for copy in round2:
        copy.wait_send()
    for copy in round3:
        copy.wait()
    sum_ref[...] = total[...]


def finish(conv_ref, grad_ref, sum_ref, conv_hbm, grad_hbm, wg_hbm, wg_ref, sems):
    conv_copy = pltpu.make_async_copy(conv_ref, conv_hbm, sems.at[0])
    grad_copy = pltpu.make_async_copy(grad_ref, grad_hbm, sems.at[1])
    conv_copy.start()
    grad_copy.start()
    for h in range(2):
        turned = sum_ref[128 * h : 128 * h + 128, :].T
        for at in range(4):
            ab = 4 * h + at
            for s in range(3):
                wg_ref[ab // 3, ab % 3, s] = turned[32 * s : 32 * s + 32, 32 * at : 32 * at + 32]
        if h == 0:
            for s in range(3):
                wg_ref[2, 2, s] = turned[96:128, 32 * s : 32 * s + 32]
    wg_copy = pltpu.make_async_copy(wg_ref, wg_hbm, sems.at[2])
    wg_copy.start()
    conv_copy.wait()
    grad_copy.wait()
    wg_copy.wait()


def local(features, brick_position, brick_count, brick_moved, weight, cotangent):
    smem = pl.BlockSpec(memory_space=pltpu.SMEM)
    vmem = pl.BlockSpec(memory_space=pltpu.VMEM)
    hbm = pl.BlockSpec(memory_space=pltpu.HBM)
    bricks = (SLOTS, SIDE, WIDTH)
    taps = (3, 3, 3, 32, 32)
    dma = pltpu.SemaphoreType.DMA
    conv, grad, summed = pl.pallas_call(
        kernel,
        out_shape=(
            pltpu.VMEM(bricks, BF),
            pltpu.VMEM(bricks, BF),
            pltpu.VMEM((256, LANES), F32),
        ),
        in_specs=[hbm, smem, smem, hbm, hbm, hbm],
        out_specs=(vmem, vmem, vmem),
        scratch_shapes=[
            pltpu.SMEM((SLOTS,), jnp.int32),
            pltpu.VMEM(bricks, BF),
            pltpu.VMEM(taps, BF),
            pltpu.VMEM((MOVE, SIDE, WIDTH), BF),
            pltpu.VMEM((MOVE, SIDE, WIDTH), BF),
            pltpu.VMEM((MOVE, SIDE, WIDTH), BF),
            pltpu.VMEM((MOVE, SIDE, WIDTH), BF),
            pltpu.VMEM(bricks, BF),
            pltpu.VMEM((2, 32, WIDTH), BF),
            pltpu.VMEM((2, CENTRE, WIDTH), BF),
            pltpu.VMEM((2, 2, CAND, LANES), BF),
            pltpu.VMEM((6, 8, LANES), F32),
            pltpu.VMEM((2, 2, 8, LANES), F32),
            pltpu.VMEM((2, 8, LANES), F32),
            pltpu.VMEM((2, 2, 8, LANES), F32),
            pltpu.VMEM((CELLS, LANES), F32),
            pltpu.VMEM((2, 3 * CELLS, CAND), BF),
            pltpu.VMEM((2 * CELLS, CENTRE), BF),
            pltpu.VMEM((2, 3, CELLS, WIDTH + 2 * LANES), BF),
            pltpu.VMEM((3, 512, 256), BF),
            pltpu.VMEM((3, 256, 512), BF),
            pltpu.VMEM((256, LANES), F32),
            pltpu.VMEM((NEAR, CHUNK, LANES), F32),
            pltpu.VMEM((CHUNK, LANES), F32),
            pltpu.VMEM((FAR, CHUNK, LANES), F32),
            pltpu.VMEM((256, LANES), F32),
            dma((4,)),
            dma((2, 8)),
            dma((2, 2, 8)),
            dma((2, 2, 1)),
            dma((NEAR,)),
            dma((NEAR,)),
            dma((FAR,)),
            dma((FAR,)),
            dma((NEAR,)),
            dma((NEAR,)),
            pltpu.SemaphoreType.REGULAR((2,)),
        ],
        compiler_params=pltpu.CompilerParams(
            collective_id=0, has_side_effects=True, vmem_limit_bytes=VMEM_BYTES
        ),
    )(
        pltpu.with_memory_space_constraint(brick_position, pltpu.HBM),
        brick_count,
        brick_moved,
        pltpu.with_memory_space_constraint(features.reshape(CELLS, WIDTH), pltpu.HBM),
        pltpu.with_memory_space_constraint(cotangent, pltpu.HBM),
        pltpu.with_memory_space_constraint(weight, pltpu.HBM),
    )
    return pl.pallas_call(
        finish,
        out_shape=(
            jax.ShapeDtypeStruct(bricks, BF),
            jax.ShapeDtypeStruct(bricks, BF),
            jax.ShapeDtypeStruct(taps, F32),
        ),
        in_specs=[vmem, vmem, vmem],
        out_specs=(hbm, hbm, hbm),
        scratch_shapes=[
            pltpu.VMEM(taps, F32),
            dma((3,)),
        ],
        compiler_params=pltpu.CompilerParams(vmem_limit_bytes=8 * 1024 * 1024),
    )(conv, grad, summed)


def solution(mesh):
    placed = (
        P(("gx", "gy"), None, None),
        P(("gx", "gy")),
        P(("gx", "gy")),
        P(("gx", "gy")),
        P(),
        P(("gx", "gy"), None, None),
    )
    return jax.shard_map(
        local,
        mesh=mesh,
        in_specs=placed,
        out_specs=(P(("gx", "gy"), None, None), P(("gx", "gy"), None, None), P()),
        check_vma=False,
    )
```

```python
import math

import jax
import jax.numpy as jnp
from jax import lax
from jax.experimental import pallas as pl
from jax.experimental.pallas import tpu as pltpu
from jax.sharding import PartitionSpec as P

TILE_BRICK_ROWS = 32
TILE_BRICK_COLS = 32
MOVE = 6
SLOTS = 16
SIDE = 16
CELLS = SLOTS * SIDE
WIDTH = 1024
LANES = 128
CAND = 640
CENTRE = 384
ROW_KEY = 1024.0
DEAD = -float(1 << 23)
DEAD_TARGET = -float(1 << 22)
BF = jnp.bfloat16
F32 = jnp.float32
MESH = pl.DeviceIdType.MESH
N_GX = 8
N_GY = 16
VMEM_BYTES = 49152 * 1024
NEAR = 16
FAR = 8
CHUNK = 256 // NEAR
WEST, EAST, NORTH, SOUTH = (0, -1), (0, 1), (-1, 0), (1, 0)
NORTH_WEST, NORTH_EAST, SOUTH_WEST, SOUTH_EAST = (-1, -1), (-1, 1), (1, -1), (1, 1)
STEPS = (WEST, EAST, NORTH, SOUTH, NORTH_WEST, NORTH_EAST, SOUTH_WEST, SOUTH_EAST)


def twice(steps):
    return tuple((2 * row, 2 * col) for row, col in steps)


def dot(a, b):
    return jnp.dot(a, b, preferred_element_type=F32)


def kernel(
    pos_hbm,
    count_ref,
    moved_ref,
    x_hbm,
    c_hbm,
    w_hbm,
    conv_ref,
    grad_ref,
    sum_ref,
    pos_ref,
    c_ref,
    w_ref,
    lent,
    borrowed,
    lent_y,
    borrowed_y,
    y_ref,
    strips,
    cand_c,
    cand_s,
    key_send,
    key_side,
    key_edge,
    key_corner,
    col_key,
    hot_s,
    hot_c,
    wide,
    guest_g,
    guest_x,
    outer,
    band_f,
    band_b,
    part,
    inbox1,
    mine,
    inbox2,
    total,
    in_sems,
    key_sems,
    halo_sems,
    lend_sems,
    send1,
    recv1,
    send2,
    recv2,
    send3,
    recv3,
    ready,
):
    gx = lax.axis_index("gx")
    gy = lax.axis_index("gy")

    fetches = [
        pltpu.make_async_copy(src, dst, in_sems.at[at])
        for at, (src, dst) in enumerate(
            (
                (c_hbm, c_ref),
                (x_hbm, cand_c.at[0, pl.ds(0, CELLS), :]),
                (w_hbm, w_ref),
                (pos_hbm, pos_ref),
            )
        )
    ]
    for at in (3, 0, 1, 2):
        fetches[at].start()

    def there(step):
        row, col = gx + step[0], gy + step[1]
        return (row >= 0) & (row < N_GX) & (col >= 0) & (col < N_GY)

    def place(step):
        return jnp.clip(gx + step[0], 0, N_GX - 1), jnp.clip(gy + step[1], 0, N_GY - 1)

    def back(step):
        return -step[0], -step[1]

    def how_many(steps):
        return sum(jnp.where(there(step), 1, 0) for step in steps)

    def signal(semaphore, peer):
        pl.semaphore_signal(semaphore, inc=1, device_id=peer, device_id_type=MESH)

    def signal_steps(semaphore, steps):
        for step in steps:

            @pl.when(there(step))
            def _(step=step):
                signal(semaphore, place(step))

    x_lo, z = lax.rem(gx, 2), lax.div(gx, 2)
    x_hi, y, core = lax.div(gy, 8), lax.rem(lax.div(gy, 2), 4), lax.rem(gy, 2)

    def flip(bit, do):
        return 1 - bit if do else bit

    def flip2(value, by):
        low, high = lax.rem(value, 2), lax.div(value, 2)
        return flip(low, by % 2) + 2 * flip(high, by // 2)

    def near(k):
        to = (flip(x_lo, k & 1), flip(x_hi, k >> 1 & 1), flip(core, k >> 2 & 1))
        low = flip(lax.rem(z, 2), k >> 3)
        rank = to[0] + 2 * to[1] + 4 * to[2] + 8 * low
        return (4 * lax.div(z, 2) + 2 * low + to[0], 8 * to[1] + 2 * y + to[2]), rank

    def far(k):
        return (2 * flip2(z, 2 * (k & 1)) + x_lo, 8 * x_hi + 2 * flip2(y, k >> 1) + core)

    my_near = x_lo + 2 * x_hi + 4 * core + 8 * lax.rem(z, 2)
    my_far = lax.div(z, 2) + 2 * y
    partner = near(2)[0]

    @pl.when(how_many(STEPS) < len(STEPS))
    def _():
        key_side[...] = jnp.full(key_side.shape, DEAD, F32)
        key_edge[...] = jnp.full(key_edge.shape, DEAD, F32)
        key_corner[...] = jnp.full(key_corner.shape, DEAD, F32)
        for field in range(2):
            cand_c[field, CELLS : CELLS + 32, :] = jnp.zeros((32, WIDTH), BF)
            for s in range(2):
                cand_s[field, s, CELLS : 2 * CELLS + 64, :] = jnp.zeros((CELLS + 64, LANES), BF)

    barrier = pltpu.get_barrier_semaphore()
    far_side = [near(k)[0] for k in range(1, NEAR)]
    for peer in far_side:
        signal(barrier, peer)
    signal_steps(barrier, STEPS)

    fetches[3].wait()
    count = count_ref[0]
    moved = moved_ref[0]
    kept = count - moved

    fetches[0].wait()
    for j in range(MOVE):
        lent[j] = c_ref[jnp.clip(kept + j, 0, SLOTS - 1)]

    sub = lax.broadcasted_iota(jnp.int32, (SIDE, LANES), 0)
    lane = lax.broadcasted_iota(jnp.int32, (8, CELLS), 1)
    lane_edge = lax.broadcasted_iota(jnp.int32, (8, LANES), 1)
    row_key = jnp.full((8, CELLS), DEAD, F32)
    north_key = jnp.full((8, LANES), DEAD, F32)
    for i in range(SLOTS):
        at = pos_ref[i]
        at = jnp.clip(at, 0, TILE_BRICK_ROWS * TILE_BRICK_COLS - 1)
        brick_row = gx * TILE_BRICK_ROWS + lax.shift_right_logical(at, 5)
        brick_col = gy * TILE_BRICK_COLS + lax.bitwise_and(at, 31)
        key = brick_row * (SIDE * 1024) + brick_col
        live = i < count
        target = jnp.where(live, key, int(DEAD_TARGET))
        source = jnp.where(live, key, int(DEAD))
        col_key[i * SIDE : (i + 1) * SIDE, :] = (sub * 1024 + target).astype(F32)
        wide_key = (jnp.zeros((8, CELLS), jnp.int32) + source).astype(F32)
        row_key = jnp.where(lax.shift_right_logical(lane, 4) == i, wide_key, row_key)
        north_key = jnp.where(
            lax.bitwise_and(lane_edge, 15) == i, wide_key[:, :LANES], north_key
        )
    row_key = row_key + lax.bitwise_and(lane, 15).astype(F32) * ROW_KEY
    south_key = north_key + (SIDE - 1) * ROW_KEY
    dead = jnp.full((8, LANES), DEAD, F32)

    def between(low, value):
        return jnp.where((lane_edge >= low) & (lane_edge < low + 16), value, dead)

    key_send[0] = row_key[:, :LANES]
    key_send[1] = row_key[:, LANES:]
    key_send[2] = between(0, south_key)
    key_send[3] = between(16, north_key)
    key_send[4] = between(32, south_key)
    key_send[5] = between(48, north_key)

    pick_row = lax.broadcasted_iota(jnp.int32, (32, CELLS), 0)
    pick_col = lax.broadcasted_iota(jnp.int32, (32, CELLS), 1)
    picked = lax.bitwise_and(pick_row, 15) * SIDE + lax.shift_right_logical(pick_row, 4) * 15
    pick = jnp.where(pick_col == picked, 1.0, 0.0).astype(BF)
    fetches[1].wait()
    strips[0] = dot(pick, cand_c[0, :CELLS, :]).astype(BF)


    pl.semaphore_wait(barrier, how_many(STEPS) + len(far_side))

    def remote(src, dst, sems, at, peer):
        return pltpu.make_async_remote_copy(
            src_ref=src,
            dst_ref=dst,
            send_sem=sems.at[0, at],
            recv_sem=sems.at[1, at],
            device_id=peer,
            device_id_type=MESH,
        )

    def halo(field, bricks):
        last = pl.ds(WIDTH - LANES, LANES)
        first = pl.ds(0, LANES)
        n_rows, s_rows = pl.ds(0, 16), pl.ds(16, 16)
        edge_n, edge_s = pl.ds(CELLS, 16), pl.ds(CELLS + 16, 16)
        corner_n, corner_s = pl.ds(2 * CELLS + 32, 16), pl.ds(2 * CELLS + 48, 16)
        side = pl.ds(CELLS, CELLS)
        own = bricks
        s = strips.at[field]
        c = cand_c.at[field]
        left, right = cand_s.at[field, 0], cand_s.at[field, 1]
        plan = [
            (own.at[:, first], right.at[side, :], WEST),
            (own.at[:, last], left.at[side, :], EAST),
            (s.at[n_rows, :], c.at[edge_s, :], NORTH),
            (s.at[s_rows, :], c.at[edge_n, :], SOUTH),
            (s.at[n_rows, first], right.at[corner_s, :], NORTH_WEST),
            (s.at[n_rows, last], left.at[corner_s, :], NORTH_EAST),
            (s.at[s_rows, first], right.at[corner_n, :], SOUTH_WEST),
            (s.at[s_rows, last], left.at[corner_n, :], SOUTH_EAST),
        ]
        return [
            (remote(src, dst, halo_sems.at[field], at, place(step)), step)
            for at, (src, dst, step) in enumerate(plan)
        ]

    def start_all(copies):
        for copy, step in copies:

            @pl.when(there(step))
            def _(copy=copy):
                copy.start()

    def wait_all(copies):
        for copy, step in copies:

            @pl.when(there(back(step)))
            def _(copy=copy):
                copy.wait_recv()

            @pl.when(there(step))
            def _(copy=copy):
                copy.wait_send()

    lend = remote(lent, borrowed, lend_sems.at[0], 0, partner)
    row = pl.ds(0, 1)
    key_plan = [
        (key_send.at[pl.ds(0, 2), row], key_side.at[1, :, row], WEST),
        (key_send.at[pl.ds(0, 2), row], key_side.at[0, :, row], EAST),
        (key_send.at[3, row], key_edge.at[1, row], NORTH),
        (key_send.at[2, row], key_edge.at[0, row], SOUTH),
        (key_send.at[5, row], key_corner.at[1, 1, row], NORTH_WEST),
        (key_send.at[5, row], key_corner.at[0, 1, row], NORTH_EAST),
        (key_send.at[4, row], key_corner.at[1, 0, row], SOUTH_WEST),
        (key_send.at[4, row], key_corner.at[0, 0, row], SOUTH_EAST),
    ]
    keys = [
        (remote(src, dst, key_sems, at, place(step)), step)
        for at, (src, dst, step) in enumerate(key_plan)
    ]
    start_all(keys)
    x_halo = halo(0, cand_c.at[0, pl.ds(0, CELLS)])
    start_all(x_halo)
    lend.start()

    def side_hot(s, tiles):
        for a in range(3):
            target = col_key[...] + ((a - 1) * ROW_KEY + (2 * s - 1))
            for t, candidate in tiles:
                hot = jnp.where(target == candidate, 1.0, 0.0).astype(BF)
                hot_s[s, a * CELLS : (a + 1) * CELLS, t * LANES : (t + 1) * LANES] = hot

    def centre_hot(tiles):
        for at, a in enumerate((0, 2)):
            target = col_key[...] + (a - 1) * ROW_KEY
            for t, candidate in tiles:
                hot = jnp.where(target == candidate, 1.0, 0.0).astype(BF)
                hot_c[at * CELLS : (at + 1) * CELLS, t * LANES : (t + 1) * LANES] = hot

    own_tiles = [(0, key_send[0, :1]), (1, key_send[1, :1])]
    for s in range(2):
        side_hot(s, own_tiles)
    centre_hot(own_tiles)

    for field in range(2):
        cand_c[field, CELLS + 32 :, :] = jnp.zeros((CENTRE - CELLS - 32, WIDTH), BF)
        for s in range(2):
            cand_s[field, s, 2 * CELLS + 64 :, :] = jnp.zeros((CAND - 2 * CELLS - 64, LANES), BF)

    fetches[2].wait()
    def strip_of(a, frame_in):
        blocks = []
        for b in (2, 1, 0):
            for frame_out in (0, 1):
                blocks.append(w_ref[a, b, frame_in - frame_out + 1].astype(F32))
        z = jnp.zeros((32, 256), F32)
        return jnp.concatenate([z] + blocks + [z], axis=1)

    for a in range(3):
        for frame_in in range(2):
            strip = strip_of(a, frame_in)
            at = 32 * frame_in
            for q in range(1, 7):
                start = 448 - 64 * q
                band_f[a, 64 * q + at : 64 * q + at + 32, :] = strip[
                    :, start : start + 256
                ].astype(BF)
            for q in (0, 7):
                band_f[a, 64 * q + at : 64 * q + at + 32, :] = jnp.zeros((32, 256), BF)
            for j in range(4):
                start = 192 - 64 * j
                band_b[2 - a, 64 * j + at : 64 * j + at + 32, :] = strip[
                    :, start : start + 512
                ].astype(BF)

    wait_all(keys)
    signal_steps(ready.at[0], twice(STEPS))
    edge_key = jnp.maximum(key_edge[0, :1], key_edge[1, :1])
    for s in range(2):
        corner_key = jnp.maximum(key_corner[s, 0, :1], key_corner[s, 1, :1])
        tail_key = jnp.maximum(edge_key, corner_key)
        side_hot(s, [(2, key_side[s, 0, :1]), (3, key_side[s, 1, :1]), (4, tail_key)])
    centre_hot([(2, edge_key)])

    def widen(field):
        c = cand_c.at[field]
        for s, (start, to) in enumerate(((WIDTH - LANES, 0), (0, WIDTH + LANES))):
            cs = cand_s.at[field, s]
            cs[:CELLS, :] = c[:CELLS, start : start + LANES]
            cs[2 * CELLS : 2 * CELLS + 32, :] = c[CELLS : CELLS + 32, start : start + LANES]
            found = dot(hot_s[s], cs[...]).astype(BF)
            for a in range(3):
                wide[field, a, :, :, to : to + LANES] = found[a * CELLS : (a + 1) * CELLS].reshape(
                    SLOTS, SIDE, LANES
                )
        found = dot(hot_c[...], c[...]).astype(BF)
        shape = (SLOTS, SIDE, WIDTH)
        wide[field, 0, :, :, LANES : LANES + WIDTH] = found[:CELLS].reshape(shape)
        wide[field, 1, :, :, LANES : LANES + WIDTH] = c[:CELLS, :].reshape(shape)
        wide[field, 2, :, :, LANES : LANES + WIDTH] = found[CELLS:].reshape(shape)

    def window(field, a, group):
        return wide[field, a, :, :, 256 * group : 256 * group + 512].reshape(CELLS, 512)

    wait_all(x_halo)
    widen(0)

    for i in range(SLOTS):
        own = c_ref[i]
        cand_c[1, i * SIDE : (i + 1) * SIDE, :] = lax.select(i < kept, own, jnp.zeros_like(own))
    flipped = cand_c[1, :CELLS, :].T
    for a in range(3):
        value = jnp.zeros((256, 512), F32)
        for group in range(4):
            value = value + dot(flipped[256 * group : 256 * group + 256, :], window(0, a, group))
        outer[a] = value
    for j in range(MOVE):
        for a in range(3):
            guest_x[a, j * SIDE : (j + 1) * SIDE, :] = wide[0, a, jnp.clip(kept + j, 0, SLOTS - 1)]
    for a in range(3):
        guest_x[a, MOVE * SIDE :, :] = jnp.zeros((LANES - MOVE * SIDE, WIDTH + 2 * LANES), BF)
    guest_g[MOVE * SIDE :, :] = jnp.zeros((LANES - MOVE * SIDE, WIDTH), BF)

    pl.semaphore_wait(ready.at[0], how_many(twice(STEPS)))
    signal_steps(ready.at[1], twice(twice(STEPS)))

    lend.wait()
    for j in range(MOVE):
        guest = borrowed[j]
        guest_g[j * SIDE : (j + 1) * SIDE, :] = lax.select(j < moved, guest, jnp.zeros_like(guest))
    flipped = guest_g[...].T
    low = lax.broadcasted_iota(jnp.int32, (32, LANES), 1)
    keep = low < 64
    blocks = []
    for a in range(3):
        both_parts = outer[a]
        for group in range(4):
            both_parts = both_parts + dot(
                flipped[256 * group : 256 * group + 256, :],
                guest_x[a, :, 256 * group : 256 * group + 512],
            )
        for b in range(3):
            sums = [jnp.zeros((64, LANES), F32), jnp.zeros((64, LANES), F32)]
            for j in range(4):
                column = j + b + 1
                tile = column // 2
                sums[column % 2] = (
                    sums[column % 2]
                    + both_parts[64 * j : 64 * j + 64, LANES * tile : LANES * tile + LANES]
                )
            both = sums[0] + pltpu.roll(sums[1], 64, 1)
            top = jnp.where(keep, both[:32], 0.0)
            bottom = jnp.where(keep, both[32:], 0.0)
            blocks.append(bottom + pltpu.roll(top, 32, 1))
    ninth = blocks[8]
    for s in range(3):
        piece = jnp.where((low >= 32 * s) & (low < 32 * s + 32), ninth, 0.0)
        blocks[s] = blocks[s] + pltpu.roll(piece, 96 - 32 * s, 1)
    for ab in range(8):
        part[32 * ab : 32 * ab + 32, :] = blocks[ab]

    round1 = []
    for k in range(1, NEAR):
        peer, rank = near(k)
        round1.append(
            pltpu.make_async_remote_copy(
                src_ref=part.at[pl.ds(pl.multiple_of(rank * CHUNK, CHUNK), CHUNK), :],
                dst_ref=inbox1.at[k],
                send_sem=send1.at[k],
                recv_sem=recv1.at[k],
                device_id=peer,
                device_id_type=MESH,
            )
        )
    for copy in round1:
        copy.start()

    for i in range(SLOTS):
        guest = borrowed[jnp.clip(i - kept, 0, MOVE - 1)]
        value = lax.select(
            i < kept, c_ref[i], lax.select(i < count, guest, jnp.zeros_like(guest))
        )
        cand_c[1, i * SIDE : (i + 1) * SIDE, :] = value
    strips[1] = dot(pick, cand_c[1, :CELLS, :]).astype(BF)
    g_halo = halo(1, cand_c.at[1, pl.ds(0, CELLS)])
    start_all(g_halo)

    def convolve(field, apply):
        for group in range(4):
            value = jnp.zeros((CELLS, 256), F32)
            for a in range(3):
                value = value + apply(a, window(field, a, group))
            yield group, value

    slot_row = lax.broadcasted_iota(jnp.int32, (CELLS, 256), 0)
    live_rows = slot_row < count * SIDE
    for group, value in convolve(0, lambda a, rows: dot(rows, band_f[a])):
        value = jnp.where(live_rows, value, 0.0).astype(BF)
        y_ref[:, :, 256 * group : 256 * group + 256] = value.reshape(SLOTS, SIDE, 256)
    for j in range(MOVE):
        brick = y_ref[jnp.clip(kept + j, 0, SLOTS - 1)]
        lent_y[j] = lax.select(j < moved, brick, jnp.zeros_like(brick))
    lend_y = remote(lent_y, borrowed_y, lend_sems.at[1], 0, partner)

    for copy in round1:
        copy.wait_recv()
    own_chunk = pl.ds(pl.multiple_of(my_near * CHUNK, CHUNK), CHUNK)
    own_rows = part[own_chunk, :]
    for k in range(1, NEAR):
        own_rows = own_rows + inbox1[k]
    mine[...] = own_rows
    inbox2[my_far] = own_rows
    pl.semaphore_wait(ready.at[1], how_many(twice(twice(STEPS))))
    round2 = []
    for k in range(1, FAR):
        round2.append(
            pltpu.make_async_remote_copy(
                src_ref=mine,
                dst_ref=inbox2.at[my_far],
                send_sem=send2.at[k],
                recv_sem=recv2.at[k],
                device_id=far(k),
                device_id_type=MESH,
            )
        )
    for copy in round2:
        copy.start()

    lend_y.start()

    wait_all(g_halo)
    widen(1)
    by_rows = (((1,), (1,)), ((), ()))
    for group, value in convolve(
        1,
        lambda a, rows: lax.dot_general(rows, band_b[a], by_rows, preferred_element_type=F32),
    ):
        value = jnp.where(live_rows, value, 0.0).astype(BF)
        grad_ref[:, :, 256 * group : 256 * group + 256] = value.reshape(SLOTS, SIDE, 256)

    for copy in round2:
        copy.wait_recv()
    chunk_sum = inbox2[0]
    for k in range(1, FAR):
        chunk_sum = chunk_sum + inbox2[k]
    total[own_chunk, :] = chunk_sum * (1.0 / math.sqrt(N_GX * N_GY * SLOTS * SIDE * SIDE * 2))
    round3 = []
    for k in range(1, NEAR):
        round3.append(
            pltpu.make_async_remote_copy(
                src_ref=total.at[own_chunk, :],
                dst_ref=total.at[own_chunk, :],
                send_sem=send3.at[k],
                recv_sem=recv3.at[k],
                device_id=near(k)[0],
                device_id_type=MESH,
            )
        )
    for copy in round3:
        copy.start()

    lend_y.wait()
    for i in range(SLOTS):
        guest = borrowed_y[jnp.clip(i - kept, 0, MOVE - 1)]
        guest = lax.select(i < kept + MOVE, guest, jnp.zeros_like(guest))
        conv_ref[i] = lax.select(i < kept, y_ref[i], guest)

    for copy in round1:
        copy.wait_send()
    for copy in round2:
        copy.wait_send()
    for copy in round3:
        copy.wait()
    sum_ref[...] = total[...]


def finish(conv_ref, grad_ref, sum_ref, conv_hbm, grad_hbm, wg_hbm, wg_ref, sems):
    conv_copy = pltpu.make_async_copy(conv_ref, conv_hbm, sems.at[0])
    grad_copy = pltpu.make_async_copy(grad_ref, grad_hbm, sems.at[1])
    conv_copy.start()
    grad_copy.start()
    for h in range(2):
        turned = sum_ref[128 * h : 128 * h + 128, :].T
        for at in range(4):
            ab = 4 * h + at
            for s in range(3):
                wg_ref[ab // 3, ab % 3, s] = turned[32 * s : 32 * s + 32, 32 * at : 32 * at + 32]
        if h == 0:
            for s in range(3):
                wg_ref[2, 2, s] = turned[96:128, 32 * s : 32 * s + 32]
    wg_copy = pltpu.make_async_copy(wg_ref, wg_hbm, sems.at[2])
    wg_copy.start()
    conv_copy.wait()
    grad_copy.wait()
    wg_copy.wait()


def local(features, brick_position, brick_count, brick_moved, weight, cotangent):
    smem = pl.BlockSpec(memory_space=pltpu.SMEM)
    vmem = pl.BlockSpec(memory_space=pltpu.VMEM)
    hbm = pl.BlockSpec(memory_space=pltpu.HBM)
    bricks = (SLOTS, SIDE, WIDTH)
    taps = (3, 3, 3, 32, 32)
    dma = pltpu.SemaphoreType.DMA
    conv, grad, summed = pl.pallas_call(
        kernel,
        out_shape=(
            pltpu.VMEM(bricks, BF),
            pltpu.VMEM(bricks, BF),
            pltpu.VMEM((256, LANES), F32),
        ),
        in_specs=[hbm, smem, smem, hbm, hbm, hbm],
        out_specs=(vmem, vmem, vmem),
        scratch_shapes=[
            pltpu.SMEM((SLOTS,), jnp.int32),
            pltpu.VMEM(bricks, BF),
            pltpu.VMEM(taps, BF),
            pltpu.VMEM((MOVE, SIDE, WIDTH), BF),
            pltpu.VMEM((MOVE, SIDE, WIDTH), BF),
            pltpu.VMEM((MOVE, SIDE, WIDTH), BF),
            pltpu.VMEM((MOVE, SIDE, WIDTH), BF),
            pltpu.VMEM(bricks, BF),
            pltpu.VMEM((2, 32, WIDTH), BF),
            pltpu.VMEM((2, CENTRE, WIDTH), BF),
            pltpu.VMEM((2, 2, CAND, LANES), BF),
            pltpu.VMEM((6, 8, LANES), F32),
            pltpu.VMEM((2, 2, 8, LANES), F32),
            pltpu.VMEM((2, 8, LANES), F32),
            pltpu.VMEM((2, 2, 8, LANES), F32),
            pltpu.VMEM((CELLS, LANES), F32),
            pltpu.VMEM((2, 3 * CELLS, CAND), BF),
            pltpu.VMEM((2 * CELLS, CENTRE), BF),
            pltpu.VMEM((2, 3, SLOTS, SIDE, WIDTH + 2 * LANES), BF),
            pltpu.VMEM((LANES, WIDTH), BF),
            pltpu.VMEM((3, LANES, WIDTH + 2 * LANES), BF),
            pltpu.VMEM((3, 256, 512), F32),
            pltpu.VMEM((3, 512, 256), BF),
            pltpu.VMEM((3, 256, 512), BF),
            pltpu.VMEM((256, LANES), F32),
            pltpu.VMEM((NEAR, CHUNK, LANES), F32),
            pltpu.VMEM((CHUNK, LANES), F32),
            pltpu.VMEM((FAR, CHUNK, LANES), F32),
            pltpu.VMEM((256, LANES), F32),
            dma((4,)),
            dma((2, 8)),
            dma((2, 2, 8)),
            dma((2, 2, 1)),
            dma((NEAR,)),
            dma((NEAR,)),
            dma((FAR,)),
            dma((FAR,)),
            dma((NEAR,)),
            dma((NEAR,)),
            pltpu.SemaphoreType.REGULAR((2,)),
        ],
        compiler_params=pltpu.CompilerParams(
            collective_id=0, has_side_effects=True, vmem_limit_bytes=VMEM_BYTES
        ),
    )(
        pltpu.with_memory_space_constraint(brick_position, pltpu.HBM),
        brick_count,
        brick_moved,
        pltpu.with_memory_space_constraint(features.reshape(CELLS, WIDTH), pltpu.HBM),
        pltpu.with_memory_space_constraint(cotangent, pltpu.HBM),
        pltpu.with_memory_space_constraint(weight, pltpu.HBM),
    )
    return pl.pallas_call(
        finish,
        out_shape=(
            jax.ShapeDtypeStruct(bricks, BF),
            jax.ShapeDtypeStruct(bricks, BF),
            jax.ShapeDtypeStruct(taps, F32),
        ),
        in_specs=[vmem, vmem, vmem],
        out_specs=(hbm, hbm, hbm),
        scratch_shapes=[
            pltpu.VMEM(taps, F32),
            dma((3,)),
        ],
        compiler_params=pltpu.CompilerParams(vmem_limit_bytes=8 * 1024 * 1024),
    )(conv, grad, summed)


def solution(mesh):
    placed = (
        P(("gx", "gy"), None, None),
        P(("gx", "gy")),
        P(("gx", "gy")),
        P(("gx", "gy")),
        P(),
        P(("gx", "gy"), None, None),
    )
    return jax.shard_map(
        local,
        mesh=mesh,
        in_specs=placed,
        out_specs=(P(("gx", "gy"), None, None), P(("gx", "gy"), None, None), P()),
        check_vma=False,
    )
```

```python
import math

import jax
import jax.numpy as jnp
from jax import lax
from jax.experimental import pallas as pl
from jax.experimental.pallas import tpu as pltpu
from jax.sharding import PartitionSpec as P

TILE_BRICK_ROWS = 32
TILE_BRICK_COLS = 32
MOVE = 6
SLOTS = 16
SIDE = 16
CELLS = SLOTS * SIDE
WIDTH = 1024
LANES = 128
CAND = 640
CENTRE = 384
ROW_KEY = 1024.0
DEAD = -float(1 << 23)
DEAD_TARGET = -float(1 << 22)
BF = jnp.bfloat16
F32 = jnp.float32
MESH = pl.DeviceIdType.MESH
N_GX = 8
N_GY = 16
VMEM_BYTES = 49152 * 1024
NEAR = 16
FAR = 8
CHUNK = 256 // NEAR
WEST, EAST, NORTH, SOUTH = (0, -1), (0, 1), (-1, 0), (1, 0)
NORTH_WEST, NORTH_EAST, SOUTH_WEST, SOUTH_EAST = (-1, -1), (-1, 1), (1, -1), (1, 1)
STEPS = (WEST, EAST, NORTH, SOUTH, NORTH_WEST, NORTH_EAST, SOUTH_WEST, SOUTH_EAST)


def twice(steps):
    return tuple((2 * row, 2 * col) for row, col in steps)


def dot(a, b):
    return jnp.dot(a, b, preferred_element_type=F32)


def kernel(
    pos_hbm,
    moved_ref,
    x_hbm,
    c_hbm,
    w_hbm,
    conv_ref,
    grad_ref,
    sum_ref,
    pos_ref,
    c_ref,
    w_ref,
    lent,
    borrowed,
    lent_y,
    borrowed_y,
    y_ref,
    strips,
    cand_c,
    cand_s,
    key_send,
    key_side,
    key_edge,
    key_corner,
    col_key,
    hot_s,
    hot_c,
    wide,
    guest_g,
    guest_x,
    outer,
    band_f,
    band_b,
    part,
    inbox1,
    mine,
    inbox2,
    total,
    in_sems,
    key_sems,
    halo_sems,
    lend_sems,
    send1,
    recv1,
    send2,
    recv2,
    send3,
    recv3,
    ready,
):
    gx = lax.axis_index("gx")
    gy = lax.axis_index("gy")

    def there(step):
        row, col = gx + step[0], gy + step[1]
        return (row >= 0) & (row < N_GX) & (col >= 0) & (col < N_GY)

    def place(step):
        return jnp.clip(gx + step[0], 0, N_GX - 1), jnp.clip(gy + step[1], 0, N_GY - 1)

    def back(step):
        return -step[0], -step[1]

    def how_many(steps):
        return sum(jnp.where(there(step), 1, 0) for step in steps)

    def signal(semaphore, peer):
        pl.semaphore_signal(semaphore, inc=1, device_id=peer, device_id_type=MESH)

    def signal_steps(semaphore, steps):
        for step in steps:

            @pl.when(there(step))
            def _(step=step):
                signal(semaphore, place(step))

    x_lo, z = lax.rem(gx, 2), lax.div(gx, 2)
    x_hi, y, core = lax.div(gy, 8), lax.rem(lax.div(gy, 2), 4), lax.rem(gy, 2)

    def flip(bit, do):
        return 1 - bit if do else bit

    def flip2(value, by):
        low, high = lax.rem(value, 2), lax.div(value, 2)
        return flip(low, by % 2) + 2 * flip(high, by // 2)

    def near(k):
        to = (flip(x_lo, k & 1), flip(x_hi, k >> 1 & 1), flip(core, k >> 2 & 1))
        low = flip(lax.rem(z, 2), k >> 3)
        rank = to[0] + 2 * to[1] + 4 * to[2] + 8 * low
        return (4 * lax.div(z, 2) + 2 * low + to[0], 8 * to[1] + 2 * y + to[2]), rank

    def far(k):
        return (2 * flip2(z, 2 * (k & 1)) + x_lo, 8 * x_hi + 2 * flip2(y, k >> 1) + core)

    my_near = x_lo + 2 * x_hi + 4 * core + 8 * lax.rem(z, 2)
    my_far = lax.div(z, 2) + 2 * y
    partner = near(2)[0]

    @pl.when(how_many(STEPS) < len(STEPS))
    def _():
        key_side[...] = jnp.full(key_side.shape, DEAD, F32)
        key_edge[...] = jnp.full(key_edge.shape, DEAD, F32)
        key_corner[...] = jnp.full(key_corner.shape, DEAD, F32)
        for field in range(2):
            cand_c[field, CELLS : CELLS + 32, :] = jnp.zeros((32, WIDTH), BF)
            for s in range(2):
                cand_s[field, s, CELLS : 2 * CELLS + 64, :] = jnp.zeros((CELLS + 64, LANES), BF)

    barrier = pltpu.get_barrier_semaphore()
    far_side = [near(k)[0] for k in (2, 3, 6, 7)]
    for peer in far_side:
        signal(barrier, peer)
    signal_steps(barrier, STEPS)

    fetches = [
        pltpu.make_async_copy(src, dst, in_sems.at[at])
        for at, (src, dst) in enumerate(
            (
                (c_hbm, c_ref),
                (x_hbm, cand_c.at[0, pl.ds(0, CELLS), :]),
                (w_hbm, w_ref),
                (pos_hbm, pos_ref),
            )
        )
    ]
    for at in (3, 0, 1, 2):
        fetches[at].start()

    fetches[3].wait()
    count = sum(jnp.where(pos_ref[i] >= 0, 1, 0) for i in range(SLOTS))
    moved = moved_ref[0]
    kept = count - moved

    sub = lax.broadcasted_iota(jnp.int32, (SIDE, LANES), 0)
    lane = lax.broadcasted_iota(jnp.int32, (8, CELLS), 1)
    lane_edge = lax.broadcasted_iota(jnp.int32, (8, LANES), 1)
    row_key = jnp.full((8, CELLS), DEAD, F32)
    north_key = jnp.full((8, LANES), DEAD, F32)
    for i in range(SLOTS):
        at = pos_ref[i]
        at = jnp.clip(at, 0, TILE_BRICK_ROWS * TILE_BRICK_COLS - 1)
        brick_row = gx * TILE_BRICK_ROWS + lax.shift_right_logical(at, 5)
        brick_col = gy * TILE_BRICK_COLS + lax.bitwise_and(at, 31)
        key = brick_row * (SIDE * 1024) + brick_col
        live = i < count
        target = jnp.where(live, key, int(DEAD_TARGET))
        source = jnp.where(live, key, int(DEAD))
        col_key[i * SIDE : (i + 1) * SIDE, :] = (sub * 1024 + target).astype(F32)
        wide_key = (jnp.zeros((8, CELLS), jnp.int32) + source).astype(F32)
        row_key = jnp.where(lax.shift_right_logical(lane, 4) == i, wide_key, row_key)
        north_key = jnp.where(
            lax.bitwise_and(lane_edge, 15) == i, wide_key[:, :LANES], north_key
        )
    row_key = row_key + lax.bitwise_and(lane, 15).astype(F32) * ROW_KEY
    south_key = north_key + (SIDE - 1) * ROW_KEY
    dead = jnp.full((8, LANES), DEAD, F32)

    def between(low, value):
        return jnp.where((lane_edge >= low) & (lane_edge < low + 16), value, dead)

    key_send[0] = row_key[:, :LANES]
    key_send[1] = row_key[:, LANES:]
    key_send[2] = between(0, south_key)
    key_send[3] = between(16, north_key)
    key_send[4] = between(32, south_key)
    key_send[5] = between(48, north_key)

    pick_row = lax.broadcasted_iota(jnp.int32, (32, CELLS), 0)
    pick_col = lax.broadcasted_iota(jnp.int32, (32, CELLS), 1)
    picked = lax.bitwise_and(pick_row, 15) * SIDE + lax.shift_right_logical(pick_row, 4) * 15
    pick = jnp.where(pick_col == picked, 1.0, 0.0).astype(BF)
    fetches[1].wait()
    strips[0] = dot(pick, cand_c[0, :CELLS, :]).astype(BF)


    pl.semaphore_wait(barrier, how_many(STEPS) + len(far_side))

    def remote(src, dst, sems, at, peer):
        return pltpu.make_async_remote_copy(
            src_ref=src,
            dst_ref=dst,
            send_sem=sems.at[0, at],
            recv_sem=sems.at[1, at],
            device_id=peer,
            device_id_type=MESH,
        )

    def halo(field, bricks):
        last = pl.ds(WIDTH - LANES, LANES)
        first = pl.ds(0, LANES)
        n_rows, s_rows = pl.ds(0, 16), pl.ds(16, 16)
        edge_n, edge_s = pl.ds(CELLS, 16), pl.ds(CELLS + 16, 16)
        corner_n, corner_s = pl.ds(2 * CELLS + 32, 16), pl.ds(2 * CELLS + 48, 16)
        side = pl.ds(CELLS, CELLS)
        own = bricks
        s = strips.at[field]
        c = cand_c.at[field]
        left, right = cand_s.at[field, 0], cand_s.at[field, 1]
        plan = [
            (own.at[:, first], right.at[side, :], WEST),
            (own.at[:, last], left.at[side, :], EAST),
            (s.at[n_rows, :], c.at[edge_s, :], NORTH),
            (s.at[s_rows, :], c.at[edge_n, :], SOUTH),
            (s.at[n_rows, first], right.at[corner_s, :], NORTH_WEST),
            (s.at[n_rows, last], left.at[corner_s, :], NORTH_EAST),
            (s.at[s_rows, first], right.at[corner_n, :], SOUTH_WEST),
            (s.at[s_rows, last], left.at[corner_n, :], SOUTH_EAST),
        ]
        return [
            (remote(src, dst, halo_sems.at[field], at, place(step)), step)
            for at, (src, dst, step) in enumerate(plan)
        ]

    def start_all(copies):
        for copy, step in copies:

            @pl.when(there(step))
            def _(copy=copy):
                copy.start()

    def wait_all(copies):
        for copy, step in copies:

            @pl.when(there(back(step)))
            def _(copy=copy):
                copy.wait_recv()

            @pl.when(there(step))
            def _(copy=copy):
                copy.wait_send()

    lend = remote(lent, borrowed, lend_sems.at[0], 0, partner)
    row = pl.ds(0, 1)
    key_plan = [
        (key_send.at[pl.ds(0, 2), row], key_side.at[1, :, row], WEST),
        (key_send.at[pl.ds(0, 2), row], key_side.at[0, :, row], EAST),
        (key_send.at[3, row], key_edge.at[1, row], NORTH),
        (key_send.at[2, row], key_edge.at[0, row], SOUTH),
        (key_send.at[5, row], key_corner.at[1, 1, row], NORTH_WEST),
        (key_send.at[5, row], key_corner.at[0, 1, row], NORTH_EAST),
        (key_send.at[4, row], key_corner.at[1, 0, row], SOUTH_WEST),
        (key_send.at[4, row], key_corner.at[0, 0, row], SOUTH_EAST),
    ]
    keys = [
        (remote(src, dst, key_sems, at, place(step)), step)
        for at, (src, dst, step) in enumerate(key_plan)
    ]
    start_all(keys)
    x_halo = halo(0, cand_c.at[0, pl.ds(0, CELLS)])
    start_all(x_halo)
    fetches[0].wait()
    for j in range(MOVE):
        lent[j] = c_ref[jnp.clip(kept + j, 0, SLOTS - 1)]
    lend.start()

    def side_hot(s, tiles):
        for a in range(3):
            target = col_key[...] + ((a - 1) * ROW_KEY + (2 * s - 1))
            for t, candidate in tiles:
                hot = jnp.where(target == candidate, 1.0, 0.0).astype(BF)
                hot_s[s, a * CELLS : (a + 1) * CELLS, t * LANES : (t + 1) * LANES] = hot

    def centre_hot(tiles):
        for at, a in enumerate((0, 2)):
            target = col_key[...] + (a - 1) * ROW_KEY
            for t, candidate in tiles:
                hot = jnp.where(target == candidate, 1.0, 0.0).astype(BF)
                hot_c[at * CELLS : (at + 1) * CELLS, t * LANES : (t + 1) * LANES] = hot

    own_tiles = [(0, key_send[0, :1]), (1, key_send[1, :1])]
    for s in range(2):
        side_hot(s, own_tiles)
    centre_hot(own_tiles)

    for field in range(2):
        cand_c[field, CELLS + 32 :, :] = jnp.zeros((CENTRE - CELLS - 32, WIDTH), BF)
        for s in range(2):
            cand_s[field, s, 2 * CELLS + 64 :, :] = jnp.zeros((CAND - 2 * CELLS - 64, LANES), BF)

    fetches[2].wait()
    def strip_of(a, frame_in):
        blocks = []
        for b in (2, 1, 0):
            for frame_out in (0, 1):
                blocks.append(w_ref[a, b, frame_in - frame_out + 1].astype(F32))
        z = jnp.zeros((32, 256), F32)
        return jnp.concatenate([z] + blocks + [z], axis=1)

    for a in range(3):
        for frame_in in range(2):
            strip = strip_of(a, frame_in)
            at = 32 * frame_in
            for q in range(1, 7):
                start = 448 - 64 * q
                band_f[a, 64 * q + at : 64 * q + at + 32, :] = strip[
                    :, start : start + 256
                ].astype(BF)
            for q in (0, 7):
                band_f[a, 64 * q + at : 64 * q + at + 32, :] = jnp.zeros((32, 256), BF)
            for j in range(4):
                start = 192 - 64 * j
                band_b[2 - a, 64 * j + at : 64 * j + at + 32, :] = strip[
                    :, start : start + 512
                ].astype(BF)

    wait_all(keys)
    signal_steps(ready.at[0], twice(STEPS))
    edge_key = jnp.maximum(key_edge[0, :1], key_edge[1, :1])
    for s in range(2):
        corner_key = jnp.maximum(key_corner[s, 0, :1], key_corner[s, 1, :1])
        tail_key = jnp.maximum(edge_key, corner_key)
        side_hot(s, [(2, key_side[s, 0, :1]), (3, key_side[s, 1, :1]), (4, tail_key)])
    centre_hot([(2, edge_key)])

    def widen(field):
        c = cand_c.at[field]
        for s, (start, to) in enumerate(((WIDTH - LANES, 0), (0, WIDTH + LANES))):
            cs = cand_s.at[field, s]
            cs[:CELLS, :] = c[:CELLS, start : start + LANES]
            cs[2 * CELLS : 2 * CELLS + 32, :] = c[CELLS : CELLS + 32, start : start + LANES]
            found = dot(hot_s[s], cs[...]).astype(BF)
            for a in range(3):
                wide[field, a, :, :, to : to + LANES] = found[a * CELLS : (a + 1) * CELLS].reshape(
                    SLOTS, SIDE, LANES
                )
        found = dot(hot_c[...], c[...]).astype(BF)
        shape = (SLOTS, SIDE, WIDTH)
        wide[field, 0, :, :, LANES : LANES + WIDTH] = found[:CELLS].reshape(shape)
        wide[field, 1, :, :, LANES : LANES + WIDTH] = c[:CELLS, :].reshape(shape)
        wide[field, 2, :, :, LANES : LANES + WIDTH] = found[CELLS:].reshape(shape)

    def window(field, a, group):
        return wide[field, a, :, :, 256 * group : 256 * group + 512].reshape(CELLS, 512)

    wait_all(x_halo)
    widen(0)

    for i in range(SLOTS):
        own = c_ref[i]
        cand_c[1, i * SIDE : (i + 1) * SIDE, :] = lax.select(i < kept, own, jnp.zeros_like(own))
    flipped = cand_c[1, :CELLS, :].T
    for a in range(3):
        value = jnp.zeros((256, 512), F32)
        for group in range(4):
            value = value + dot(flipped[256 * group : 256 * group + 256, :], window(0, a, group))
        outer[a] = value
    for j in range(MOVE):
        for a in range(3):
            guest_x[a, j * SIDE : (j + 1) * SIDE, :] = wide[0, a, jnp.clip(kept + j, 0, SLOTS - 1)]
    for a in range(3):
        guest_x[a, MOVE * SIDE :, :] = jnp.zeros((LANES - MOVE * SIDE, WIDTH + 2 * LANES), BF)
    guest_g[MOVE * SIDE :, :] = jnp.zeros((LANES - MOVE * SIDE, WIDTH), BF)

    pl.semaphore_wait(ready.at[0], how_many(twice(STEPS)))
    signal_steps(ready.at[1], twice(twice(STEPS)))

    lend.wait()
    for j in range(MOVE):
        guest = borrowed[j]
        guest_g[j * SIDE : (j + 1) * SIDE, :] = lax.select(j < moved, guest, jnp.zeros_like(guest))
    flipped = guest_g[...].T
    low = lax.broadcasted_iota(jnp.int32, (32, LANES), 1)
    keep = low < 64
    blocks = []
    for a in range(3):
        both_parts = outer[a]
        for group in range(4):
            both_parts = both_parts + dot(
                flipped[256 * group : 256 * group + 256, :],
                guest_x[a, :, 256 * group : 256 * group + 512],
            )
        for b in range(3):
            sums = [jnp.zeros((64, LANES), F32), jnp.zeros((64, LANES), F32)]
            for j in range(4):
                column = j + b + 1
                tile = column // 2
                sums[column % 2] = (
                    sums[column % 2]
                    + both_parts[64 * j : 64 * j + 64, LANES * tile : LANES * tile + LANES]
                )
            both = sums[0] + pltpu.roll(sums[1], 64, 1)
            top = jnp.where(keep, both[:32], 0.0)
            bottom = jnp.where(keep, both[32:], 0.0)
            blocks.append(bottom + pltpu.roll(top, 32, 1))
    ninth = blocks[8]
    for s in range(3):
        piece = jnp.where((low >= 32 * s) & (low < 32 * s + 32), ninth, 0.0)
        blocks[s] = blocks[s] + pltpu.roll(piece, 96 - 32 * s, 1)
    for ab in range(8):
        part[32 * ab : 32 * ab + 32, :] = blocks[ab]

    round1 = []
    for k in range(1, NEAR):
        peer, rank = near(k)
        round1.append(
            pltpu.make_async_remote_copy(
                src_ref=part.at[pl.ds(pl.multiple_of(rank * CHUNK, CHUNK), CHUNK), :],
                dst_ref=inbox1.at[k],
                send_sem=send1.at[k],
                recv_sem=recv1.at[k],
                device_id=peer,
                device_id_type=MESH,
            )
        )
    for copy in round1:
        copy.start()

    for i in range(SLOTS):
        guest = borrowed[jnp.clip(i - kept, 0, MOVE - 1)]
        value = lax.select(
            i < kept, c_ref[i], lax.select(i < count, guest, jnp.zeros_like(guest))
        )
        cand_c[1, i * SIDE : (i + 1) * SIDE, :] = value
    strips[1] = dot(pick, cand_c[1, :CELLS, :]).astype(BF)
    g_halo = halo(1, cand_c.at[1, pl.ds(0, CELLS)])
    start_all(g_halo)

    def convolve(field, apply):
        for group in range(4):
            value = jnp.zeros((CELLS, 256), F32)
            for a in range(3):
                value = value + apply(a, window(field, a, group))
            yield group, value

    slot_row = lax.broadcasted_iota(jnp.int32, (CELLS, 256), 0)
    live_rows = slot_row < count * SIDE
    for group, value in convolve(0, lambda a, rows: dot(rows, band_f[a])):
        value = jnp.where(live_rows, value, 0.0).astype(BF)
        y_ref[:, :, 256 * group : 256 * group + 256] = value.reshape(SLOTS, SIDE, 256)
    for j in range(MOVE):
        brick = y_ref[jnp.clip(kept + j, 0, SLOTS - 1)]
        lent_y[j] = lax.select(j < moved, brick, jnp.zeros_like(brick))
    lend_y = remote(lent_y, borrowed_y, lend_sems.at[1], 0, partner)

    for copy in round1:
        copy.wait_recv()
    own_chunk = pl.ds(pl.multiple_of(my_near * CHUNK, CHUNK), CHUNK)
    own_rows = part[own_chunk, :]
    for k in range(1, NEAR):
        own_rows = own_rows + inbox1[k]
    mine[...] = own_rows
    inbox2[my_far] = own_rows
    pl.semaphore_wait(ready.at[1], how_many(twice(twice(STEPS))))
    round2 = []
    for k in range(1, FAR):
        round2.append(
            pltpu.make_async_remote_copy(
                src_ref=mine,
                dst_ref=inbox2.at[my_far],
                send_sem=send2.at[k],
                recv_sem=recv2.at[k],
                device_id=far(k),
                device_id_type=MESH,
            )
        )
    for copy in round2:
        copy.start()

    lend_y.start()

    wait_all(g_halo)
    widen(1)
    by_rows = (((1,), (1,)), ((), ()))
    for group, value in convolve(
        1,
        lambda a, rows: lax.dot_general(rows, band_b[a], by_rows, preferred_element_type=F32),
    ):
        value = jnp.where(live_rows, value, 0.0).astype(BF)
        grad_ref[:, :, 256 * group : 256 * group + 256] = value.reshape(SLOTS, SIDE, 256)

    for copy in round2:
        copy.wait_recv()
    chunk_sum = inbox2[0]
    for k in range(1, FAR):
        chunk_sum = chunk_sum + inbox2[k]
    total[own_chunk, :] = chunk_sum * (1.0 / math.sqrt(N_GX * N_GY * SLOTS * SIDE * SIDE * 2))
    round3 = []
    for k in range(1, NEAR):
        round3.append(
            pltpu.make_async_remote_copy(
                src_ref=total.at[own_chunk, :],
                dst_ref=total.at[own_chunk, :],
                send_sem=send3.at[k],
                recv_sem=recv3.at[k],
                device_id=near(k)[0],
                device_id_type=MESH,
            )
        )
    for copy in round3:
        copy.start()

    lend_y.wait()
    for i in range(SLOTS):
        guest = borrowed_y[jnp.clip(i - kept, 0, MOVE - 1)]
        guest = lax.select(i < kept + MOVE, guest, jnp.zeros_like(guest))
        conv_ref[i] = lax.select(i < kept, y_ref[i], guest)

    for copy in round1:
        copy.wait_send()
    for copy in round2:
        copy.wait_send()
    for copy in round3:
        copy.wait()
    sum_ref[...] = total[...]


def finish(conv_ref, grad_ref, sum_ref, conv_hbm, grad_hbm, wg_hbm, wg_ref, sems):
    conv_copy = pltpu.make_async_copy(conv_ref, conv_hbm, sems.at[0])
    grad_copy = pltpu.make_async_copy(grad_ref, grad_hbm, sems.at[1])
    conv_copy.start()
    grad_copy.start()
    for h in range(2):
        turned = sum_ref[128 * h : 128 * h + 128, :].T
        for at in range(4):
            ab = 4 * h + at
            for s in range(3):
                wg_ref[ab // 3, ab % 3, s] = turned[32 * s : 32 * s + 32, 32 * at : 32 * at + 32]
        if h == 0:
            for s in range(3):
                wg_ref[2, 2, s] = turned[96:128, 32 * s : 32 * s + 32]
    wg_copy = pltpu.make_async_copy(wg_ref, wg_hbm, sems.at[2])
    wg_copy.start()
    conv_copy.wait()
    grad_copy.wait()
    wg_copy.wait()


def local(features, brick_position, brick_count, brick_moved, weight, cotangent):
    smem = pl.BlockSpec(memory_space=pltpu.SMEM)
    vmem = pl.BlockSpec(memory_space=pltpu.VMEM)
    hbm = pl.BlockSpec(memory_space=pltpu.HBM)
    bricks = (SLOTS, SIDE, WIDTH)
    taps = (3, 3, 3, 32, 32)
    dma = pltpu.SemaphoreType.DMA
    conv, grad, summed = pl.pallas_call(
        kernel,
        out_shape=(
            pltpu.VMEM(bricks, BF),
            pltpu.VMEM(bricks, BF),
            pltpu.VMEM((256, LANES), F32),
        ),
        in_specs=[hbm, smem, hbm, hbm, hbm],
        out_specs=(vmem, vmem, vmem),
        scratch_shapes=[
            pltpu.SMEM((SLOTS,), jnp.int32),
            pltpu.VMEM(bricks, BF),
            pltpu.VMEM(taps, BF),
            pltpu.VMEM((MOVE, SIDE, WIDTH), BF),
            pltpu.VMEM((MOVE, SIDE, WIDTH), BF),
            pltpu.VMEM((MOVE, SIDE, WIDTH), BF),
            pltpu.VMEM((MOVE, SIDE, WIDTH), BF),
            pltpu.VMEM(bricks, BF),
            pltpu.VMEM((2, 32, WIDTH), BF),
            pltpu.VMEM((2, CENTRE, WIDTH), BF),
            pltpu.VMEM((2, 2, CAND, LANES), BF),
            pltpu.VMEM((6, 8, LANES), F32),
            pltpu.VMEM((2, 2, 8, LANES), F32),
            pltpu.VMEM((2, 8, LANES), F32),
            pltpu.VMEM((2, 2, 8, LANES), F32),
            pltpu.VMEM((CELLS, LANES), F32),
            pltpu.VMEM((2, 3 * CELLS, CAND), BF),
            pltpu.VMEM((2 * CELLS, CENTRE), BF),
            pltpu.VMEM((2, 3, SLOTS, SIDE, WIDTH + 2 * LANES), BF),
            pltpu.VMEM((LANES, WIDTH), BF),
            pltpu.VMEM((3, LANES, WIDTH + 2 * LANES), BF),
            pltpu.VMEM((3, 256, 512), F32),
            pltpu.VMEM((3, 512, 256), BF),
            pltpu.VMEM((3, 256, 512), BF),
            pltpu.VMEM((256, LANES), F32),
            pltpu.VMEM((NEAR, CHUNK, LANES), F32),
            pltpu.VMEM((CHUNK, LANES), F32),
            pltpu.VMEM((FAR, CHUNK, LANES), F32),
            pltpu.VMEM((256, LANES), F32),
            dma((4,)),
            dma((2, 8)),
            dma((2, 2, 8)),
            dma((2, 2, 1)),
            dma((NEAR,)),
            dma((NEAR,)),
            dma((FAR,)),
            dma((FAR,)),
            dma((NEAR,)),
            dma((NEAR,)),
            pltpu.SemaphoreType.REGULAR((2,)),
        ],
        compiler_params=pltpu.CompilerParams(
            collective_id=0, has_side_effects=True, vmem_limit_bytes=VMEM_BYTES
        ),
    )(
        pltpu.with_memory_space_constraint(brick_position, pltpu.HBM),
        brick_moved,
        pltpu.with_memory_space_constraint(features.reshape(CELLS, WIDTH), pltpu.HBM),
        pltpu.with_memory_space_constraint(cotangent, pltpu.HBM),
        pltpu.with_memory_space_constraint(weight, pltpu.HBM),
    )
    return pl.pallas_call(
        finish,
        out_shape=(
            jax.ShapeDtypeStruct(bricks, BF),
            jax.ShapeDtypeStruct(bricks, BF),
            jax.ShapeDtypeStruct(taps, F32),
        ),
        in_specs=[vmem, vmem, vmem],
        out_specs=(hbm, hbm, hbm),
        scratch_shapes=[
            pltpu.VMEM(taps, F32),
            dma((3,)),
        ],
        compiler_params=pltpu.CompilerParams(vmem_limit_bytes=8 * 1024 * 1024),
    )(conv, grad, summed)


def solution(mesh):
    placed = (
        P(("gx", "gy"), None, None),
        P(("gx", "gy")),
        P(("gx", "gy")),
        P(("gx", "gy")),
        P(),
        P(("gx", "gy"), None, None),
    )
    return jax.shard_map(
        local,
        mesh=mesh,
        in_specs=placed,
        out_specs=(P(("gx", "gy"), None, None), P(("gx", "gy"), None, None), P()),
        check_vma=False,
    )
```

```python
import math

import jax
import jax.numpy as jnp
from jax import lax
from jax.experimental import pallas as pl
from jax.experimental.pallas import tpu as pltpu
from jax.sharding import PartitionSpec as P

TILE_BRICK_ROWS = 32
TILE_BRICK_COLS = 32
MOVE = 6
SLOTS = 16
SIDE = 16
CELLS = SLOTS * SIDE
WIDTH = 1024
LANES = 128
CAND = 640
CENTRE = 384
ROW_KEY = 1024.0
DEAD = -float(1 << 23)
DEAD_TARGET = -float(1 << 22)
BF = jnp.bfloat16
F32 = jnp.float32
MESH = pl.DeviceIdType.MESH
N_GX = 8
N_GY = 16
VMEM_BYTES = 49152 * 1024
NEAR = 16
FAR = 8
CHUNK = 256 // NEAR
WEST, EAST, NORTH, SOUTH = (0, -1), (0, 1), (-1, 0), (1, 0)
NORTH_WEST, NORTH_EAST, SOUTH_WEST, SOUTH_EAST = (-1, -1), (-1, 1), (1, -1), (1, 1)
STEPS = (NORTH_WEST, NORTH_EAST, SOUTH_WEST, SOUTH_EAST, NORTH, SOUTH, WEST, EAST)
NEAR_ORDER = (10, 14, 11, 15, 2, 6, 3, 7, 9, 13, 8, 12, 1, 5, 4)
FAR_ORDER = (5, 7, 4, 6, 3, 1, 2)


def twice(steps):
    return tuple((2 * row, 2 * col) for row, col in steps)


def dot(a, b):
    return jnp.dot(a, b, preferred_element_type=F32)


def kernel(
    pos_hbm,
    moved_ref,
    x_hbm,
    c_hbm,
    w_hbm,
    conv_ref,
    grad_ref,
    sum_ref,
    pos_ref,
    c_ref,
    w_ref,
    lent,
    borrowed,
    lent_y,
    borrowed_y,
    y_ref,
    strips,
    cand_c,
    cand_s,
    key_send,
    key_side,
    key_edge,
    key_corner,
    col_key,
    hot_s,
    hot_c,
    wide,
    guest_g,
    guest_x,
    outer,
    band_f,
    band_b,
    part,
    inbox1,
    mine,
    inbox2,
    total,
    in_sems,
    key_sems,
    halo_sems,
    lend_sems,
    send1,
    recv1,
    send2,
    recv2,
    send3,
    recv3,
    ready,
):
    gx = lax.axis_index("gx")
    gy = lax.axis_index("gy")

    def there(step):
        row, col = gx + step[0], gy + step[1]
        return (row >= 0) & (row < N_GX) & (col >= 0) & (col < N_GY)

    def place(step):
        return jnp.clip(gx + step[0], 0, N_GX - 1), jnp.clip(gy + step[1], 0, N_GY - 1)

    def back(step):
        return -step[0], -step[1]

    def how_many(steps):
        return sum(jnp.where(there(step), 1, 0) for step in steps)

    def signal(semaphore, peer):
        pl.semaphore_signal(semaphore, inc=1, device_id=peer, device_id_type=MESH)

    def signal_steps(semaphore, steps):
        for step in steps:

            @pl.when(there(step))
            def _(step=step):
                signal(semaphore, place(step))

    x_lo, z = lax.rem(gx, 2), lax.div(gx, 2)
    x_hi, y, core = lax.div(gy, 8), lax.rem(lax.div(gy, 2), 4), lax.rem(gy, 2)

    def flip(bit, do):
        return 1 - bit if do else bit

    def flip2(value, by):
        low, high = lax.rem(value, 2), lax.div(value, 2)
        return flip(low, by % 2) + 2 * flip(high, by // 2)

    def near(k):
        to = (flip(x_lo, k & 1), flip(x_hi, k >> 1 & 1), flip(core, k >> 2 & 1))
        low = flip(lax.rem(z, 2), k >> 3)
        rank = to[0] + 2 * to[1] + 4 * to[2] + 8 * low
        return (4 * lax.div(z, 2) + 2 * low + to[0], 8 * to[1] + 2 * y + to[2]), rank

    def far(k):
        return (2 * flip2(z, 2 * (k & 1)) + x_lo, 8 * x_hi + 2 * flip2(y, k >> 1) + core)

    my_near = x_lo + 2 * x_hi + 4 * core + 8 * lax.rem(z, 2)
    my_far = lax.div(z, 2) + 2 * y
    partner = near(2)[0]

    @pl.when(how_many(STEPS) < len(STEPS))
    def _():
        key_side[...] = jnp.full(key_side.shape, DEAD, F32)
        key_edge[...] = jnp.full(key_edge.shape, DEAD, F32)
        key_corner[...] = jnp.full(key_corner.shape, DEAD, F32)
        for field in range(2):
            cand_c[field, CELLS : CELLS + 32, :] = jnp.zeros((32, WIDTH), BF)
            for s in range(2):
                cand_s[field, s, CELLS : 2 * CELLS + 64, :] = jnp.zeros((CELLS + 64, LANES), BF)

    barrier = pltpu.get_barrier_semaphore()
    far_side = [near(k)[0] for k in (2, 3, 6, 7)]
    for peer in far_side:
        signal(barrier, peer)
    signal_steps(barrier, STEPS)

    fetches = [
        pltpu.make_async_copy(src, dst, in_sems.at[at])
        for at, (src, dst) in enumerate(
            (
                (c_hbm, c_ref),
                (x_hbm, cand_c.at[0, pl.ds(0, CELLS), :]),
                (w_hbm, w_ref),
                (pos_hbm, pos_ref),
            )
        )
    ]
    for at in (3, 0, 1, 2):
        fetches[at].start()

    fetches[3].wait()
    count = sum(jnp.where(pos_ref[i] >= 0, 1, 0) for i in range(SLOTS))
    moved = moved_ref[0]
    kept = count - moved

    sub = lax.broadcasted_iota(jnp.int32, (SIDE, LANES), 0)
    lane = lax.broadcasted_iota(jnp.int32, (8, CELLS), 1)
    lane_edge = lax.broadcasted_iota(jnp.int32, (8, LANES), 1)
    row_key = jnp.full((8, CELLS), DEAD, F32)
    north_key = jnp.full((8, LANES), DEAD, F32)
    for i in range(SLOTS):
        at = pos_ref[i]
        at = jnp.clip(at, 0, TILE_BRICK_ROWS * TILE_BRICK_COLS - 1)
        brick_row = gx * TILE_BRICK_ROWS + lax.shift_right_logical(at, 5)
        brick_col = gy * TILE_BRICK_COLS + lax.bitwise_and(at, 31)
        key = brick_row * (SIDE * 1024) + brick_col
        live = i < count
        target = jnp.where(live, key, int(DEAD_TARGET))
        source = jnp.where(live, key, int(DEAD))
        col_key[i * SIDE : (i + 1) * SIDE, :] = (sub * 1024 + target).astype(F32)
        wide_key = (jnp.zeros((8, CELLS), jnp.int32) + source).astype(F32)
        row_key = jnp.where(lax.shift_right_logical(lane, 4) == i, wide_key, row_key)
        north_key = jnp.where(
            lax.bitwise_and(lane_edge, 15) == i, wide_key[:, :LANES], north_key
        )
    row_key = row_key + lax.bitwise_and(lane, 15).astype(F32) * ROW_KEY
    south_key = north_key + (SIDE - 1) * ROW_KEY
    dead = jnp.full((8, LANES), DEAD, F32)

    def between(low, value):
        return jnp.where((lane_edge >= low) & (lane_edge < low + 16), value, dead)

    key_send[0] = row_key[:, :LANES]
    key_send[1] = row_key[:, LANES:]
    key_send[2] = between(0, south_key)
    key_send[3] = between(16, north_key)
    key_send[4] = between(32, south_key)
    key_send[5] = between(48, north_key)

    pick_row = lax.broadcasted_iota(jnp.int32, (32, CELLS), 0)
    pick_col = lax.broadcasted_iota(jnp.int32, (32, CELLS), 1)
    picked = lax.bitwise_and(pick_row, 15) * SIDE + lax.shift_right_logical(pick_row, 4) * 15
    pick = jnp.where(pick_col == picked, 1.0, 0.0).astype(BF)
    fetches[1].wait()
    strips[0] = dot(pick, cand_c[0, :CELLS, :]).astype(BF)


    pl.semaphore_wait(barrier, how_many(STEPS) + len(far_side))

    def remote(src, dst, sems, at, peer):
        return pltpu.make_async_remote_copy(
            src_ref=src,
            dst_ref=dst,
            send_sem=sems.at[0, at],
            recv_sem=sems.at[1, at],
            device_id=peer,
            device_id_type=MESH,
        )

    def halo(field, bricks):
        last = pl.ds(WIDTH - LANES, LANES)
        first = pl.ds(0, LANES)
        n_rows, s_rows = pl.ds(0, 16), pl.ds(16, 16)
        edge_n, edge_s = pl.ds(CELLS, 16), pl.ds(CELLS + 16, 16)
        corner_n, corner_s = pl.ds(2 * CELLS + 32, 16), pl.ds(2 * CELLS + 48, 16)
        side = pl.ds(CELLS, CELLS)
        own = bricks
        s = strips.at[field]
        c = cand_c.at[field]
        left, right = cand_s.at[field, 0], cand_s.at[field, 1]
        plan = [
            (own.at[:, first], right.at[side, :], WEST),
            (own.at[:, last], left.at[side, :], EAST),
            (s.at[n_rows, :], c.at[edge_s, :], NORTH),
            (s.at[s_rows, :], c.at[edge_n, :], SOUTH),
            (s.at[n_rows, first], right.at[corner_s, :], NORTH_WEST),
            (s.at[n_rows, last], left.at[corner_s, :], NORTH_EAST),
            (s.at[s_rows, first], right.at[corner_n, :], SOUTH_WEST),
            (s.at[s_rows, last], left.at[corner_n, :], SOUTH_EAST),
        ]
        return [
            (remote(src, dst, halo_sems.at[field], at, place(step)), step)
            for at, (src, dst, step) in enumerate(plan)
        ]

    def start_all(copies):
        for copy, step in copies:

            @pl.when(there(step))
            def _(copy=copy):
                copy.start()

    def wait_all(copies):
        for copy, step in copies:

            @pl.when(there(back(step)))
            def _(copy=copy):
                copy.wait_recv()

    def wait_sent(copies):
        for copy, step in copies:

            @pl.when(there(step))
            def _(copy=copy):
                copy.wait_send()

    lend = remote(lent, borrowed, lend_sems.at[0], 0, partner)
    row = pl.ds(0, 1)
    key_plan = [
        (key_send.at[pl.ds(0, 2), row], key_side.at[1, :, row], WEST),
        (key_send.at[pl.ds(0, 2), row], key_side.at[0, :, row], EAST),
        (key_send.at[3, row], key_edge.at[1, row], NORTH),
        (key_send.at[2, row], key_edge.at[0, row], SOUTH),
        (key_send.at[5, row], key_corner.at[1, 1, row], NORTH_WEST),
        (key_send.at[5, row], key_corner.at[0, 1, row], NORTH_EAST),
        (key_send.at[4, row], key_corner.at[1, 0, row], SOUTH_WEST),
        (key_send.at[4, row], key_corner.at[0, 0, row], SOUTH_EAST),
    ]
    keys = [
        (remote(src, dst, key_sems, at, place(step)), step)
        for at, (src, dst, step) in enumerate(key_plan)
    ]
    start_all(keys)
    x_halo = halo(0, cand_c.at[0, pl.ds(0, CELLS)])
    start_all(x_halo)
    fetches[0].wait()
    for j in range(MOVE):
        lent[j] = c_ref[jnp.clip(kept + j, 0, SLOTS - 1)]
    lend.start()

    def side_hot(s, tiles):
        for a in range(3):
            target = col_key[...] + ((a - 1) * ROW_KEY + (2 * s - 1))
            for t, candidate in tiles:
                hot = jnp.where(target == candidate, 1.0, 0.0).astype(BF)
                hot_s[s, a * CELLS : (a + 1) * CELLS, t * LANES : (t + 1) * LANES] = hot

    def centre_hot(tiles):
        for at, a in enumerate((0, 2)):
            target = col_key[...] + (a - 1) * ROW_KEY
            for t, candidate in tiles:
                hot = jnp.where(target == candidate, 1.0, 0.0).astype(BF)
                hot_c[at * CELLS : (at + 1) * CELLS, t * LANES : (t + 1) * LANES] = hot

    own_tiles = [(0, key_send[0, :1]), (1, key_send[1, :1])]
    for s in range(2):
        side_hot(s, own_tiles)
    centre_hot(own_tiles)

    for field in range(2):
        cand_c[field, CELLS + 32 :, :] = jnp.zeros((CENTRE - CELLS - 32, WIDTH), BF)
        for s in range(2):
            cand_s[field, s, 2 * CELLS + 64 :, :] = jnp.zeros((CAND - 2 * CELLS - 64, LANES), BF)

    fetches[2].wait()
    def strip_of(a, frame_in):
        blocks = []
        for b in (2, 1, 0):
            for frame_out in (0, 1):
                blocks.append(w_ref[a, b, frame_in - frame_out + 1].astype(F32))
        z = jnp.zeros((32, 256), F32)
        return jnp.concatenate([z] + blocks + [z], axis=1)

    for a in range(3):
        for frame_in in range(2):
            strip = strip_of(a, frame_in)
            at = 32 * frame_in
            for q in range(1, 7):
                start = 448 - 64 * q
                band_f[a, 64 * q + at : 64 * q + at + 32, :] = strip[
                    :, start : start + 256
                ].astype(BF)
            for q in (0, 7):
                band_f[a, 64 * q + at : 64 * q + at + 32, :] = jnp.zeros((32, 256), BF)
            for j in range(4):
                start = 192 - 64 * j
                band_b[2 - a, 64 * j + at : 64 * j + at + 32, :] = strip[
                    :, start : start + 512
                ].astype(BF)

    wait_all(keys)
    signal_steps(ready.at[0], twice(STEPS))
    edge_key = jnp.maximum(key_edge[0, :1], key_edge[1, :1])
    for s in range(2):
        corner_key = jnp.maximum(key_corner[s, 0, :1], key_corner[s, 1, :1])
        tail_key = jnp.maximum(edge_key, corner_key)
        side_hot(s, [(2, key_side[s, 0, :1]), (3, key_side[s, 1, :1]), (4, tail_key)])
    centre_hot([(2, edge_key)])

    def widen(field):
        c = cand_c.at[field]
        for s, (start, to) in enumerate(((WIDTH - LANES, 0), (0, WIDTH + LANES))):
            cs = cand_s.at[field, s]
            cs[:CELLS, :] = c[:CELLS, start : start + LANES]
            cs[2 * CELLS : 2 * CELLS + 32, :] = c[CELLS : CELLS + 32, start : start + LANES]
            found = dot(hot_s[s], cs[...]).astype(BF)
            for a in range(3):
                wide[field, a, :, :, to : to + LANES] = found[a * CELLS : (a + 1) * CELLS].reshape(
                    SLOTS, SIDE, LANES
                )
        found = dot(hot_c[...], c[...]).astype(BF)
        shape = (SLOTS, SIDE, WIDTH)
        wide[field, 0, :, :, LANES : LANES + WIDTH] = found[:CELLS].reshape(shape)
        wide[field, 1, :, :, LANES : LANES + WIDTH] = c[:CELLS, :].reshape(shape)
        wide[field, 2, :, :, LANES : LANES + WIDTH] = found[CELLS:].reshape(shape)

    def window(field, a, group):
        return wide[field, a, :, :, 256 * group : 256 * group + 512].reshape(CELLS, 512)

    wait_all(x_halo)
    widen(0)

    for i in range(SLOTS):
        own = c_ref[i]
        cand_c[1, i * SIDE : (i + 1) * SIDE, :] = lax.select(i < kept, own, jnp.zeros_like(own))
    flipped = cand_c[1, :CELLS, :].T
    for a in range(3):
        value = jnp.zeros((256, 512), F32)
        for group in range(4):
            value = value + dot(flipped[256 * group : 256 * group + 256, :], window(0, a, group))
        outer[a] = value
    for j in range(MOVE):
        for a in range(3):
            guest_x[a, j * SIDE : (j + 1) * SIDE, :] = wide[0, a, jnp.clip(kept + j, 0, SLOTS - 1)]
    for a in range(3):
        guest_x[a, MOVE * SIDE :, :] = jnp.zeros((LANES - MOVE * SIDE, WIDTH + 2 * LANES), BF)
    guest_g[MOVE * SIDE :, :] = jnp.zeros((LANES - MOVE * SIDE, WIDTH), BF)

    pl.semaphore_wait(ready.at[0], how_many(twice(STEPS)))
    signal_steps(ready.at[1], twice(twice(STEPS)))

    lend.wait()
    for j in range(MOVE):
        guest = borrowed[j]
        guest_g[j * SIDE : (j + 1) * SIDE, :] = lax.select(j < moved, guest, jnp.zeros_like(guest))
    flipped = guest_g[...].T
    low = lax.broadcasted_iota(jnp.int32, (32, LANES), 1)
    keep = low < 64
    blocks = []
    for a in range(3):
        both_parts = outer[a]
        for group in range(4):
            both_parts = both_parts + dot(
                flipped[256 * group : 256 * group + 256, :],
                guest_x[a, :, 256 * group : 256 * group + 512],
            )
        for b in range(3):
            sums = [jnp.zeros((64, LANES), F32), jnp.zeros((64, LANES), F32)]
            for j in range(4):
                column = j + b + 1
                tile = column // 2
                sums[column % 2] = (
                    sums[column % 2]
                    + both_parts[64 * j : 64 * j + 64, LANES * tile : LANES * tile + LANES]
                )
            both = sums[0] + pltpu.roll(sums[1], 64, 1)
            top = jnp.where(keep, both[:32], 0.0)
            bottom = jnp.where(keep, both[32:], 0.0)
            blocks.append(bottom + pltpu.roll(top, 32, 1))
    ninth = blocks[8]
    for s in range(3):
        piece = jnp.where((low >= 32 * s) & (low < 32 * s + 32), ninth, 0.0)
        blocks[s] = blocks[s] + pltpu.roll(piece, 96 - 32 * s, 1)
    for ab in range(8):
        part[32 * ab : 32 * ab + 32, :] = blocks[ab]

    round1 = []
    for k in NEAR_ORDER:
        peer, rank = near(k)
        round1.append(
            pltpu.make_async_remote_copy(
                src_ref=part.at[pl.ds(pl.multiple_of(rank * CHUNK, CHUNK), CHUNK), :],
                dst_ref=inbox1.at[k],
                send_sem=send1.at[k],
                recv_sem=recv1.at[k],
                device_id=peer,
                device_id_type=MESH,
            )
        )
    for copy in round1:
        copy.start()

    for i in range(SLOTS):
        guest = borrowed[jnp.clip(i - kept, 0, MOVE - 1)]
        value = lax.select(
            i < kept, c_ref[i], lax.select(i < count, guest, jnp.zeros_like(guest))
        )
        cand_c[1, i * SIDE : (i + 1) * SIDE, :] = value
    strips[1] = dot(pick, cand_c[1, :CELLS, :]).astype(BF)
    g_halo = halo(1, cand_c.at[1, pl.ds(0, CELLS)])
    start_all(g_halo)

    def convolve(field, apply):
        for group in range(4):
            value = jnp.zeros((CELLS, 256), F32)
            for a in range(3):
                value = value + apply(a, window(field, a, group))
            yield group, value

    slot_row = lax.broadcasted_iota(jnp.int32, (CELLS, 256), 0)
    live_rows = slot_row < count * SIDE
    for group, value in convolve(0, lambda a, rows: dot(rows, band_f[a])):
        value = jnp.where(live_rows, value, 0.0).astype(BF)
        y_ref[:, :, 256 * group : 256 * group + 256] = value.reshape(SLOTS, SIDE, 256)
    for j in range(MOVE):
        brick = y_ref[jnp.clip(kept + j, 0, SLOTS - 1)]
        lent_y[j] = lax.select(j < moved, brick, jnp.zeros_like(brick))
    lend_y = remote(lent_y, borrowed_y, lend_sems.at[1], 0, partner)

    for copy in round1:
        copy.wait_recv()
    own_chunk = pl.ds(pl.multiple_of(my_near * CHUNK, CHUNK), CHUNK)
    own_rows = part[own_chunk, :]
    for k in range(1, NEAR):
        own_rows = own_rows + inbox1[k]
    mine[...] = own_rows
    inbox2[my_far] = own_rows
    pl.semaphore_wait(ready.at[1], how_many(twice(twice(STEPS))))
    round2 = []
    for k in FAR_ORDER:
        round2.append(
            pltpu.make_async_remote_copy(
                src_ref=mine,
                dst_ref=inbox2.at[my_far],
                send_sem=send2.at[k],
                recv_sem=recv2.at[k],
                device_id=far(k),
                device_id_type=MESH,
            )
        )
    for copy in round2:
        copy.start()

    lend_y.start()

    wait_all(g_halo)
    widen(1)
    by_rows = (((1,), (1,)), ((), ()))
    for group, value in convolve(
        1,
        lambda a, rows: lax.dot_general(rows, band_b[a], by_rows, preferred_element_type=F32),
    ):
        value = jnp.where(live_rows, value, 0.0).astype(BF)
        grad_ref[:, :, 256 * group : 256 * group + 256] = value.reshape(SLOTS, SIDE, 256)

    for copy in round2:
        copy.wait_recv()
    chunk_sum = inbox2[0]
    for k in range(1, FAR):
        chunk_sum = chunk_sum + inbox2[k]
    total[own_chunk, :] = chunk_sum * (1.0 / math.sqrt(N_GX * N_GY * SLOTS * SIDE * SIDE * 2))
    round3 = []
    for k in NEAR_ORDER:
        round3.append(
            pltpu.make_async_remote_copy(
                src_ref=total.at[own_chunk, :],
                dst_ref=total.at[own_chunk, :],
                send_sem=send3.at[k],
                recv_sem=recv3.at[k],
                device_id=near(k)[0],
                device_id_type=MESH,
            )
        )
    for copy in round3:
        copy.start()

    lend_y.wait()
    for i in range(SLOTS):
        guest = borrowed_y[jnp.clip(i - kept, 0, MOVE - 1)]
        guest = lax.select(i < kept + MOVE, guest, jnp.zeros_like(guest))
        conv_ref[i] = lax.select(i < kept, y_ref[i], guest)

    for copies in (keys, x_halo, g_halo):
        wait_sent(copies)
    for copy in round1:
        copy.wait_send()
    for copy in round2:
        copy.wait_send()
    for copy in round3:
        copy.wait()
    sum_ref[...] = total[...]


def finish(conv_ref, grad_ref, sum_ref, conv_hbm, grad_hbm, wg_hbm, wg_ref, sems):
    conv_copy = pltpu.make_async_copy(conv_ref, conv_hbm, sems.at[0])
    grad_copy = pltpu.make_async_copy(grad_ref, grad_hbm, sems.at[1])
    conv_copy.start()
    grad_copy.start()
    for h in range(2):
        turned = sum_ref[128 * h : 128 * h + 128, :].T
        for at in range(4):
            ab = 4 * h + at
            for s in range(3):
                wg_ref[ab // 3, ab % 3, s] = turned[32 * s : 32 * s + 32, 32 * at : 32 * at + 32]
        if h == 0:
            for s in range(3):
                wg_ref[2, 2, s] = turned[96:128, 32 * s : 32 * s + 32]
    wg_copy = pltpu.make_async_copy(wg_ref, wg_hbm, sems.at[2])
    wg_copy.start()
    conv_copy.wait()
    grad_copy.wait()
    wg_copy.wait()


def local(features, brick_position, brick_count, brick_moved, weight, cotangent):
    smem = pl.BlockSpec(memory_space=pltpu.SMEM)
    vmem = pl.BlockSpec(memory_space=pltpu.VMEM)
    hbm = pl.BlockSpec(memory_space=pltpu.HBM)
    bricks = (SLOTS, SIDE, WIDTH)
    taps = (3, 3, 3, 32, 32)
    dma = pltpu.SemaphoreType.DMA
    conv, grad, summed = pl.pallas_call(
        kernel,
        out_shape=(
            pltpu.VMEM(bricks, BF),
            pltpu.VMEM(bricks, BF),
            pltpu.VMEM((256, LANES), F32),
        ),
        in_specs=[hbm, smem, hbm, hbm, hbm],
        out_specs=(vmem, vmem, vmem),
        scratch_shapes=[
            pltpu.SMEM((SLOTS,), jnp.int32),
            pltpu.VMEM(bricks, BF),
            pltpu.VMEM(taps, BF),
            pltpu.VMEM((MOVE, SIDE, WIDTH), BF),
            pltpu.VMEM((MOVE, SIDE, WIDTH), BF),
            pltpu.VMEM((MOVE, SIDE, WIDTH), BF),
            pltpu.VMEM((MOVE, SIDE, WIDTH), BF),
            pltpu.VMEM(bricks, BF),
            pltpu.VMEM((2, 32, WIDTH), BF),
            pltpu.VMEM((2, CENTRE, WIDTH), BF),
            pltpu.VMEM((2, 2, CAND, LANES), BF),
            pltpu.VMEM((6, 8, LANES), F32),
            pltpu.VMEM((2, 2, 8, LANES), F32),
            pltpu.VMEM((2, 8, LANES), F32),
            pltpu.VMEM((2, 2, 8, LANES), F32),
            pltpu.VMEM((CELLS, LANES), F32),
            pltpu.VMEM((2, 3 * CELLS, CAND), BF),
            pltpu.VMEM((2 * CELLS, CENTRE), BF),
            pltpu.VMEM((2, 3, SLOTS, SIDE, WIDTH + 2 * LANES), BF),
            pltpu.VMEM((LANES, WIDTH), BF),
            pltpu.VMEM((3, LANES, WIDTH + 2 * LANES), BF),
            pltpu.VMEM((3, 256, 512), F32),
            pltpu.VMEM((3, 512, 256), BF),
            pltpu.VMEM((3, 256, 512), BF),
            pltpu.VMEM((256, LANES), F32),
            pltpu.VMEM((NEAR, CHUNK, LANES), F32),
            pltpu.VMEM((CHUNK, LANES), F32),
            pltpu.VMEM((FAR, CHUNK, LANES), F32),
            pltpu.VMEM((256, LANES), F32),
            dma((4,)),
            dma((2, 8)),
            dma((2, 2, 8)),
            dma((2, 2, 1)),
            dma((NEAR,)),
            dma((NEAR,)),
            dma((FAR,)),
            dma((FAR,)),
            dma((NEAR,)),
            dma((NEAR,)),
            pltpu.SemaphoreType.REGULAR((2,)),
        ],
        compiler_params=pltpu.CompilerParams(
            collective_id=0, has_side_effects=True, vmem_limit_bytes=VMEM_BYTES
        ),
    )(
        pltpu.with_memory_space_constraint(brick_position, pltpu.HBM),
        brick_moved,
        pltpu.with_memory_space_constraint(features.reshape(CELLS, WIDTH), pltpu.HBM),
        pltpu.with_memory_space_constraint(cotangent, pltpu.HBM),
        pltpu.with_memory_space_constraint(weight, pltpu.HBM),
    )
    return pl.pallas_call(
        finish,
        out_shape=(
            jax.ShapeDtypeStruct(bricks, BF),
            jax.ShapeDtypeStruct(bricks, BF),
            jax.ShapeDtypeStruct(taps, F32),
        ),
        in_specs=[vmem, vmem, vmem],
        out_specs=(hbm, hbm, hbm),
        scratch_shapes=[
            pltpu.VMEM(taps, F32),
            dma((3,)),
        ],
        compiler_params=pltpu.CompilerParams(vmem_limit_bytes=8 * 1024 * 1024),
    )(conv, grad, summed)


def solution(mesh):
    placed = (
        P(("gx", "gy"), None, None),
        P(("gx", "gy")),
        P(("gx", "gy")),
        P(("gx", "gy")),
        P(),
        P(("gx", "gy"), None, None),
    )
    return jax.shard_map(
        local,
        mesh=mesh,
        in_specs=placed,
        out_specs=(P(("gx", "gy"), None, None), P(("gx", "gy"), None, None), P()),
        check_vma=False,
    )
```

```python
import math

import jax
import jax.numpy as jnp
from jax import lax
from jax.experimental import pallas as pl
from jax.experimental.pallas import tpu as pltpu
from jax.sharding import PartitionSpec as P

TILE_BRICK_ROWS = 32
TILE_BRICK_COLS = 32
MOVE = 6
SLOTS = 16
SIDE = 16
CELLS = SLOTS * SIDE
WIDTH = 1024
LANES = 128
CAND = 640
CENTRE = 384
ROW_KEY = 1024.0
DEAD = -float(1 << 23)
DEAD_TARGET = -float(1 << 22)
BF = jnp.bfloat16
F32 = jnp.float32
MESH = pl.DeviceIdType.MESH
N_GX = 8
N_GY = 16
VMEM_BYTES = 49152 * 1024
NEAR = 16
FAR = 8
CHUNK = 256 // NEAR
WEST, EAST, NORTH, SOUTH = (0, -1), (0, 1), (-1, 0), (1, 0)
NORTH_WEST, NORTH_EAST, SOUTH_WEST, SOUTH_EAST = (-1, -1), (-1, 1), (1, -1), (1, 1)
STEPS = (NORTH_WEST, NORTH_EAST, SOUTH_WEST, SOUTH_EAST, NORTH, SOUTH, WEST, EAST)
NEAR_ORDER = (10, 14, 11, 15, 2, 6, 3, 7, 9, 13, 8, 12, 1, 5, 4)
FAR_ORDER = (5, 7, 4, 6, 3, 1, 2)


def twice(steps):
    return tuple((2 * row, 2 * col) for row, col in steps)


def dot(a, b):
    return jnp.dot(a, b, preferred_element_type=F32)


def kernel(
    pos_hbm,
    moved_ref,
    x_hbm,
    c_hbm,
    w_hbm,
    conv_ref,
    grad_ref,
    sum_ref,
    pos_ref,
    c_ref,
    w_ref,
    lent,
    borrowed,
    lent_y,
    borrowed_y,
    y_ref,
    strips,
    cand_c,
    cand_s,
    key_send,
    key_side,
    key_edge,
    key_corner,
    col_key,
    hot_s,
    hot_c,
    wide,
    guest_g,
    guest_x,
    outer,
    band_f,
    band_b,
    part,
    inbox1,
    mine,
    inbox2,
    total,
    in_sems,
    key_sems,
    halo_sems,
    lend_sems,
    send1,
    recv1,
    send2,
    recv2,
    send3,
    recv3,
    ready,
):
    gx = lax.axis_index("gx")
    gy = lax.axis_index("gy")

    def there(step):
        row, col = gx + step[0], gy + step[1]
        return (row >= 0) & (row < N_GX) & (col >= 0) & (col < N_GY)

    def place(step):
        return jnp.clip(gx + step[0], 0, N_GX - 1), jnp.clip(gy + step[1], 0, N_GY - 1)

    def back(step):
        return -step[0], -step[1]

    def how_many(steps):
        return sum(jnp.where(there(step), 1, 0) for step in steps)

    def signal(semaphore, peer):
        pl.semaphore_signal(semaphore, inc=1, device_id=peer, device_id_type=MESH)

    def signal_steps(semaphore, steps):
        for step in steps:

            @pl.when(there(step))
            def _(step=step):
                signal(semaphore, place(step))

    x_lo, z = lax.rem(gx, 2), lax.div(gx, 2)
    x_hi, y, core = lax.div(gy, 8), lax.rem(lax.div(gy, 2), 4), lax.rem(gy, 2)

    def flip(bit, do):
        return 1 - bit if do else bit

    def flip2(value, by):
        low, high = lax.rem(value, 2), lax.div(value, 2)
        return flip(low, by % 2) + 2 * flip(high, by // 2)

    def near(k):
        to = (flip(x_lo, k & 1), flip(x_hi, k >> 1 & 1), flip(core, k >> 2 & 1))
        low = flip(lax.rem(z, 2), k >> 3)
        rank = to[0] + 2 * to[1] + 4 * to[2] + 8 * low
        return (4 * lax.div(z, 2) + 2 * low + to[0], 8 * to[1] + 2 * y + to[2]), rank

    def far(k):
        return (2 * flip2(z, 2 * (k & 1)) + x_lo, 8 * x_hi + 2 * flip2(y, k >> 1) + core)

    my_near = x_lo + 2 * x_hi + 4 * core + 8 * lax.rem(z, 2)
    my_far = lax.div(z, 2) + 2 * y
    partner = near(2)[0]

    @pl.when(how_many(STEPS) < len(STEPS))
    def _():
        key_side[...] = jnp.full(key_side.shape, DEAD, F32)
        key_edge[...] = jnp.full(key_edge.shape, DEAD, F32)
        key_corner[...] = jnp.full(key_corner.shape, DEAD, F32)
        for field in range(2):
            cand_c[field, CELLS : CELLS + 32, :] = jnp.zeros((32, WIDTH), BF)
            for s in range(2):
                cand_s[field, s, CELLS : 2 * CELLS + 64, :] = jnp.zeros((CELLS + 64, LANES), BF)

    barrier = pltpu.get_barrier_semaphore()
    far_side = [near(k)[0] for k in (2, 3, 6, 7)]
    for peer in far_side:
        signal(barrier, peer)
    signal_steps(barrier, STEPS)

    fetches = [
        pltpu.make_async_copy(src, dst, in_sems.at[at])
        for at, (src, dst) in enumerate(
            (
                (c_hbm, c_ref),
                (x_hbm, cand_c.at[0, pl.ds(0, CELLS), :]),
                (w_hbm, w_ref),
                (pos_hbm, pos_ref),
            )
        )
    ]
    for at in (3, 0, 1, 2):
        fetches[at].start()

    fetches[3].wait()
    count = sum(jnp.where(pos_ref[i] >= 0, 1, 0) for i in range(SLOTS))
    moved = moved_ref[0]
    kept = count - moved

    sub = lax.broadcasted_iota(jnp.int32, (SIDE, LANES), 0)
    lane = lax.broadcasted_iota(jnp.int32, (8, CELLS), 1)
    lane_edge = lax.broadcasted_iota(jnp.int32, (8, LANES), 1)
    row_key = jnp.full((8, CELLS), DEAD, F32)
    north_key = jnp.full((8, LANES), DEAD, F32)
    for i in range(SLOTS):
        at = pos_ref[i]
        at = jnp.clip(at, 0, TILE_BRICK_ROWS * TILE_BRICK_COLS - 1)
        brick_row = gx * TILE_BRICK_ROWS + lax.shift_right_logical(at, 5)
        brick_col = gy * TILE_BRICK_COLS + lax.bitwise_and(at, 31)
        key = brick_row * (SIDE * 1024) + brick_col
        live = i < count
        target = jnp.where(live, key, int(DEAD_TARGET))
        source = jnp.where(live, key, int(DEAD))
        col_key[i * SIDE : (i + 1) * SIDE, :] = (sub * 1024 + target).astype(F32)
        wide_key = (jnp.zeros((8, CELLS), jnp.int32) + source).astype(F32)
        row_key = jnp.where(lax.shift_right_logical(lane, 4) == i, wide_key, row_key)
        north_key = jnp.where(
            lax.bitwise_and(lane_edge, 15) == i, wide_key[:, :LANES], north_key
        )
    row_key = row_key + lax.bitwise_and(lane, 15).astype(F32) * ROW_KEY
    south_key = north_key + (SIDE - 1) * ROW_KEY
    dead = jnp.full((8, LANES), DEAD, F32)

    def between(low, value):
        return jnp.where((lane_edge >= low) & (lane_edge < low + 16), value, dead)

    key_send[0] = row_key[:, :LANES]
    key_send[1] = row_key[:, LANES:]
    key_send[2] = between(0, south_key)
    key_send[3] = between(16, north_key)
    key_send[4] = between(32, south_key)
    key_send[5] = between(48, north_key)

    pick_row = lax.broadcasted_iota(jnp.int32, (32, CELLS), 0)
    pick_col = lax.broadcasted_iota(jnp.int32, (32, CELLS), 1)
    picked = lax.bitwise_and(pick_row, 15) * SIDE + lax.shift_right_logical(pick_row, 4) * 15
    pick = jnp.where(pick_col == picked, 1.0, 0.0).astype(BF)
    fetches[1].wait()
    strips[0] = dot(pick, cand_c[0, :CELLS, :]).astype(BF)


    pl.semaphore_wait(barrier, how_many(STEPS) + len(far_side))

    def remote(src, dst, sems, at, peer):
        return pltpu.make_async_remote_copy(
            src_ref=src,
            dst_ref=dst,
            send_sem=sems.at[0, at],
            recv_sem=sems.at[1, at],
            device_id=peer,
            device_id_type=MESH,
        )

    def halo(field, bricks):
        last = pl.ds(WIDTH - LANES, LANES)
        first = pl.ds(0, LANES)
        n_rows, s_rows = pl.ds(0, 16), pl.ds(16, 16)
        edge_n, edge_s = pl.ds(CELLS, 16), pl.ds(CELLS + 16, 16)
        corner_n, corner_s = pl.ds(2 * CELLS + 32, 16), pl.ds(2 * CELLS + 48, 16)
        side = pl.ds(CELLS, CELLS)
        own = bricks
        s = strips.at[field]
        c = cand_c.at[field]
        left, right = cand_s.at[field, 0], cand_s.at[field, 1]
        plan = [
            (own.at[:, first], right.at[side, :], WEST),
            (own.at[:, last], left.at[side, :], EAST),
            (s.at[n_rows, :], c.at[edge_s, :], NORTH),
            (s.at[s_rows, :], c.at[edge_n, :], SOUTH),
            (s.at[n_rows, first], right.at[corner_s, :], NORTH_WEST),
            (s.at[n_rows, last], left.at[corner_s, :], NORTH_EAST),
            (s.at[s_rows, first], right.at[corner_n, :], SOUTH_WEST),
            (s.at[s_rows, last], left.at[corner_n, :], SOUTH_EAST),
        ]
        return [
            (remote(src, dst, halo_sems.at[field], at, place(step)), step)
            for at, (src, dst, step) in enumerate(plan)
        ]

    def start_all(copies):
        for copy, step in copies:

            @pl.when(there(step))
            def _(copy=copy):
                copy.start()

    def wait_all(copies):
        for copy, step in copies:

            @pl.when(there(back(step)))
            def _(copy=copy):
                copy.wait_recv()

    def wait_sent(copies):
        for copy, step in copies:

            @pl.when(there(step))
            def _(copy=copy):
                copy.wait_send()

    lend = remote(lent, borrowed, lend_sems.at[0], 0, partner)
    row = pl.ds(0, 1)
    key_plan = [
        (key_send.at[pl.ds(0, 2), row], key_side.at[1, :, row], WEST),
        (key_send.at[pl.ds(0, 2), row], key_side.at[0, :, row], EAST),
        (key_send.at[3, row], key_edge.at[1, row], NORTH),
        (key_send.at[2, row], key_edge.at[0, row], SOUTH),
        (key_send.at[5, row], key_corner.at[1, 1, row], NORTH_WEST),
        (key_send.at[5, row], key_corner.at[0, 1, row], NORTH_EAST),
        (key_send.at[4, row], key_corner.at[1, 0, row], SOUTH_WEST),
        (key_send.at[4, row], key_corner.at[0, 0, row], SOUTH_EAST),
    ]
    keys = [
        (remote(src, dst, key_sems, at, place(step)), step)
        for at, (src, dst, step) in enumerate(key_plan)
    ]
    start_all(keys)
    fetches[0].wait()
    for j in range(MOVE):
        lent[j] = c_ref[jnp.clip(kept + j, 0, SLOTS - 1)]
    x_halo = halo(0, cand_c.at[0, pl.ds(0, CELLS)])
    start_all(x_halo)
    lend.start()

    def side_hot(s, tiles):
        for a in range(3):
            target = col_key[...] + ((a - 1) * ROW_KEY + (2 * s - 1))
            for t, candidate in tiles:
                hot = jnp.where(target == candidate, 1.0, 0.0).astype(BF)
                hot_s[s, a * CELLS : (a + 1) * CELLS, t * LANES : (t + 1) * LANES] = hot

    def centre_hot(tiles):
        for at, a in enumerate((0, 2)):
            target = col_key[...] + (a - 1) * ROW_KEY
            for t, candidate in tiles:
                hot = jnp.where(target == candidate, 1.0, 0.0).astype(BF)
                hot_c[at * CELLS : (at + 1) * CELLS, t * LANES : (t + 1) * LANES] = hot

    own_tiles = [(0, key_send[0, :1]), (1, key_send[1, :1])]
    for s in range(2):
        side_hot(s, own_tiles)
    centre_hot(own_tiles)

    for field in range(2):
        cand_c[field, CELLS + 32 :, :] = jnp.zeros((CENTRE - CELLS - 32, WIDTH), BF)
        for s in range(2):
            cand_s[field, s, 2 * CELLS + 64 :, :] = jnp.zeros((CAND - 2 * CELLS - 64, LANES), BF)

    fetches[2].wait()
    def strip_of(a, frame_in):
        blocks = []
        for b in (2, 1, 0):
            for frame_out in (0, 1):
                blocks.append(w_ref[a, b, frame_in - frame_out + 1].astype(F32))
        z = jnp.zeros((32, 256), F32)
        return jnp.concatenate([z] + blocks + [z], axis=1)

    for a in range(3):
        for frame_in in range(2):
            strip = strip_of(a, frame_in)
            at = 32 * frame_in
            for q in range(1, 7):
                start = 448 - 64 * q
                band_f[a, 64 * q + at : 64 * q + at + 32, :] = strip[
                    :, start : start + 256
                ].astype(BF)
            for q in (0, 7):
                band_f[a, 64 * q + at : 64 * q + at + 32, :] = jnp.zeros((32, 256), BF)
            for j in range(4):
                start = 192 - 64 * j
                band_b[2 - a, 64 * j + at : 64 * j + at + 32, :] = strip[
                    :, start : start + 512
                ].astype(BF)

    wait_all(keys)
    signal_steps(ready.at[0], twice(STEPS))
    edge_key = jnp.maximum(key_edge[0, :1], key_edge[1, :1])
    for s in range(2):
        corner_key = jnp.maximum(key_corner[s, 0, :1], key_corner[s, 1, :1])
        tail_key = jnp.maximum(edge_key, corner_key)
        side_hot(s, [(2, key_side[s, 0, :1]), (3, key_side[s, 1, :1]), (4, tail_key)])
    centre_hot([(2, edge_key)])

    def widen(field):
        c = cand_c.at[field]
        for s, (start, to) in enumerate(((WIDTH - LANES, 0), (0, WIDTH + LANES))):
            cs = cand_s.at[field, s]
            cs[:CELLS, :] = c[:CELLS, start : start + LANES]
            cs[2 * CELLS : 2 * CELLS + 32, :] = c[CELLS : CELLS + 32, start : start + LANES]
            found = dot(hot_s[s], cs[...]).astype(BF)
            for a in range(3):
                wide[field, a, :, :, to : to + LANES] = found[a * CELLS : (a + 1) * CELLS].reshape(
                    SLOTS, SIDE, LANES
                )
        found = dot(hot_c[...], c[...]).astype(BF)
        shape = (SLOTS, SIDE, WIDTH)
        wide[field, 0, :, :, LANES : LANES + WIDTH] = found[:CELLS].reshape(shape)
        wide[field, 1, :, :, LANES : LANES + WIDTH] = c[:CELLS, :].reshape(shape)
        wide[field, 2, :, :, LANES : LANES + WIDTH] = found[CELLS:].reshape(shape)

    def window(field, a, group):
        return wide[field, a, :, :, 256 * group : 256 * group + 512].reshape(CELLS, 512)

    wait_all(x_halo)
    widen(0)

    for i in range(SLOTS):
        own = c_ref[i]
        cand_c[1, i * SIDE : (i + 1) * SIDE, :] = lax.select(i < kept, own, jnp.zeros_like(own))
    flipped = cand_c[1, :CELLS, :].T
    for a in range(3):
        value = jnp.zeros((256, 512), F32)
        for group in range(4):
            value = value + dot(flipped[256 * group : 256 * group + 256, :], window(0, a, group))
        outer[a] = value
    for j in range(MOVE):
        for a in range(3):
            guest_x[a, j * SIDE : (j + 1) * SIDE, :] = wide[0, a, jnp.clip(kept + j, 0, SLOTS - 1)]
    for a in range(3):
        guest_x[a, MOVE * SIDE :, :] = jnp.zeros((LANES - MOVE * SIDE, WIDTH + 2 * LANES), BF)
    guest_g[MOVE * SIDE :, :] = jnp.zeros((LANES - MOVE * SIDE, WIDTH), BF)

    pl.semaphore_wait(ready.at[0], how_many(twice(STEPS)))
    signal_steps(ready.at[1], twice(twice(STEPS)))

    lend.wait()
    for j in range(MOVE):
        guest = borrowed[j]
        guest_g[j * SIDE : (j + 1) * SIDE, :] = lax.select(j < moved, guest, jnp.zeros_like(guest))
    flipped = guest_g[...].T
    low = lax.broadcasted_iota(jnp.int32, (32, LANES), 1)
    keep = low < 64
    blocks = []
    for a in range(3):
        both_parts = outer[a]
        for group in range(4):
            both_parts = both_parts + dot(
                flipped[256 * group : 256 * group + 256, :],
                guest_x[a, :, 256 * group : 256 * group + 512],
            )
        for b in range(3):
            sums = [jnp.zeros((64, LANES), F32), jnp.zeros((64, LANES), F32)]
            for j in range(4):
                column = j + b + 1
                tile = column // 2
                sums[column % 2] = (
                    sums[column % 2]
                    + both_parts[64 * j : 64 * j + 64, LANES * tile : LANES * tile + LANES]
                )
            both = sums[0] + pltpu.roll(sums[1], 64, 1)
            top = jnp.where(keep, both[:32], 0.0)
            bottom = jnp.where(keep, both[32:], 0.0)
            blocks.append(bottom + pltpu.roll(top, 32, 1))
    ninth = blocks[8]
    for s in range(3):
        piece = jnp.where((low >= 32 * s) & (low < 32 * s + 32), ninth, 0.0)
        blocks[s] = blocks[s] + pltpu.roll(piece, 96 - 32 * s, 1)
    for ab in range(8):
        part[32 * ab : 32 * ab + 32, :] = blocks[ab]

    round1 = []
    for k in NEAR_ORDER:
        peer, rank = near(k)
        round1.append(
            pltpu.make_async_remote_copy(
                src_ref=part.at[pl.ds(pl.multiple_of(rank * CHUNK, CHUNK), CHUNK), :],
                dst_ref=inbox1.at[k],
                send_sem=send1.at[k],
                recv_sem=recv1.at[k],
                device_id=peer,
                device_id_type=MESH,
            )
        )
    for copy in round1:
        copy.start()

    for i in range(SLOTS):
        guest = borrowed[jnp.clip(i - kept, 0, MOVE - 1)]
        value = lax.select(
            i < kept, c_ref[i], lax.select(i < count, guest, jnp.zeros_like(guest))
        )
        cand_c[1, i * SIDE : (i + 1) * SIDE, :] = value
    strips[1] = dot(pick, cand_c[1, :CELLS, :]).astype(BF)
    g_halo = halo(1, cand_c.at[1, pl.ds(0, CELLS)])
    start_all(g_halo)

    def convolve(field, apply):
        for group in range(4):
            value = jnp.zeros((CELLS, 256), F32)
            for a in range(3):
                value = value + apply(a, window(field, a, group))
            yield group, value

    slot_row = lax.broadcasted_iota(jnp.int32, (CELLS, 256), 0)
    live_rows = slot_row < count * SIDE
    for group, value in convolve(0, lambda a, rows: dot(rows, band_f[a])):
        value = jnp.where(live_rows, value, 0.0).astype(BF)
        y_ref[:, :, 256 * group : 256 * group + 256] = value.reshape(SLOTS, SIDE, 256)
    for j in range(MOVE):
        brick = y_ref[jnp.clip(kept + j, 0, SLOTS - 1)]
        lent_y[j] = lax.select(j < moved, brick, jnp.zeros_like(brick))
    lend_y = remote(lent_y, borrowed_y, lend_sems.at[1], 0, partner)

    for copy in round1:
        copy.wait_recv()
    own_chunk = pl.ds(pl.multiple_of(my_near * CHUNK, CHUNK), CHUNK)
    own_rows = part[own_chunk, :]
    for k in range(1, NEAR):
        own_rows = own_rows + inbox1[k]
    mine[...] = own_rows
    inbox2[my_far] = own_rows
    pl.semaphore_wait(ready.at[1], how_many(twice(twice(STEPS))))
    round2 = []
    for k in FAR_ORDER:
        round2.append(
            pltpu.make_async_remote_copy(
                src_ref=mine,
                dst_ref=inbox2.at[my_far],
                send_sem=send2.at[k],
                recv_sem=recv2.at[k],
                device_id=far(k),
                device_id_type=MESH,
            )
        )
    for copy in round2:
        copy.start()

    lend_y.start()

    wait_all(g_halo)
    widen(1)
    by_rows = (((1,), (1,)), ((), ()))
    for group, value in convolve(
        1,
        lambda a, rows: lax.dot_general(rows, band_b[a], by_rows, preferred_element_type=F32),
    ):
        value = jnp.where(live_rows, value, 0.0).astype(BF)
        grad_ref[:, :, 256 * group : 256 * group + 256] = value.reshape(SLOTS, SIDE, 256)

    for copy in round2:
        copy.wait_recv()
    chunk_sum = inbox2[0]
    for k in range(1, FAR):
        chunk_sum = chunk_sum + inbox2[k]
    total[own_chunk, :] = chunk_sum * (1.0 / math.sqrt(N_GX * N_GY * SLOTS * SIDE * SIDE * 2))
    round3 = []
    for k in NEAR_ORDER:
        round3.append(
            pltpu.make_async_remote_copy(
                src_ref=total.at[own_chunk, :],
                dst_ref=total.at[own_chunk, :],
                send_sem=send3.at[k],
                recv_sem=recv3.at[k],
                device_id=near(k)[0],
                device_id_type=MESH,
            )
        )
    for copy in round3:
        copy.start()

    lend_y.wait()
    for i in range(SLOTS):
        guest = borrowed_y[jnp.clip(i - kept, 0, MOVE - 1)]
        guest = lax.select(i < kept + MOVE, guest, jnp.zeros_like(guest))
        conv_ref[i] = lax.select(i < kept, y_ref[i], guest)

    for copies in (keys, x_halo, g_halo):
        wait_sent(copies)
    for copy in round1:
        copy.wait_send()
    for copy in round2:
        copy.wait_send()
    for copy in round3:
        copy.wait()
    sum_ref[...] = total[...]


def finish(conv_ref, grad_ref, sum_ref, conv_hbm, grad_hbm, wg_hbm, wg_ref, sems):
    conv_copy = pltpu.make_async_copy(conv_ref, conv_hbm, sems.at[0])
    grad_copy = pltpu.make_async_copy(grad_ref, grad_hbm, sems.at[1])
    conv_copy.start()
    grad_copy.start()
    for h in range(2):
        turned = sum_ref[128 * h : 128 * h + 128, :].T
        for at in range(4):
            ab = 4 * h + at
            for s in range(3):
                wg_ref[ab // 3, ab % 3, s] = turned[32 * s : 32 * s + 32, 32 * at : 32 * at + 32]
        if h == 0:
            for s in range(3):
                wg_ref[2, 2, s] = turned[96:128, 32 * s : 32 * s + 32]
    wg_copy = pltpu.make_async_copy(wg_ref, wg_hbm, sems.at[2])
    wg_copy.start()
    conv_copy.wait()
    grad_copy.wait()
    wg_copy.wait()


def local(features, brick_position, brick_count, brick_moved, weight, cotangent):
    smem = pl.BlockSpec(memory_space=pltpu.SMEM)
    vmem = pl.BlockSpec(memory_space=pltpu.VMEM)
    hbm = pl.BlockSpec(memory_space=pltpu.HBM)
    bricks = (SLOTS, SIDE, WIDTH)
    taps = (3, 3, 3, 32, 32)
    dma = pltpu.SemaphoreType.DMA
    conv, grad, summed = pl.pallas_call(
        kernel,
        out_shape=(
            pltpu.VMEM(bricks, BF),
            pltpu.VMEM(bricks, BF),
            pltpu.VMEM((256, LANES), F32),
        ),
        in_specs=[hbm, smem, hbm, hbm, hbm],
        out_specs=(vmem, vmem, vmem),
        scratch_shapes=[
            pltpu.SMEM((SLOTS,), jnp.int32),
            pltpu.VMEM(bricks, BF),
            pltpu.VMEM(taps, BF),
            pltpu.VMEM((MOVE, SIDE, WIDTH), BF),
            pltpu.VMEM((MOVE, SIDE, WIDTH), BF),
            pltpu.VMEM((MOVE, SIDE, WIDTH), BF),
            pltpu.VMEM((MOVE, SIDE, WIDTH), BF),
            pltpu.VMEM(bricks, BF),
            pltpu.VMEM((2, 32, WIDTH), BF),
            pltpu.VMEM((2, CENTRE, WIDTH), BF),
            pltpu.VMEM((2, 2, CAND, LANES), BF),
            pltpu.VMEM((6, 8, LANES), F32),
            pltpu.VMEM((2, 2, 8, LANES), F32),
            pltpu.VMEM((2, 8, LANES), F32),
            pltpu.VMEM((2, 2, 8, LANES), F32),
            pltpu.VMEM((CELLS, LANES), F32),
            pltpu.VMEM((2, 3 * CELLS, CAND), BF),
            pltpu.VMEM((2 * CELLS, CENTRE), BF),
            pltpu.VMEM((2, 3, SLOTS, SIDE, WIDTH + 2 * LANES), BF),
            pltpu.VMEM((LANES, WIDTH), BF),
            pltpu.VMEM((3, LANES, WIDTH + 2 * LANES), BF),
            pltpu.VMEM((3, 256, 512), F32),
            pltpu.VMEM((3, 512, 256), BF),
            pltpu.VMEM((3, 256, 512), BF),
            pltpu.VMEM((256, LANES), F32),
            pltpu.VMEM((NEAR, CHUNK, LANES), F32),
            pltpu.VMEM((CHUNK, LANES), F32),
            pltpu.VMEM((FAR, CHUNK, LANES), F32),
            pltpu.VMEM((256, LANES), F32),
            dma((4,)),
            dma((2, 8)),
            dma((2, 2, 8)),
            dma((2, 2, 1)),
            dma((NEAR,)),
            dma((NEAR,)),
            dma((FAR,)),
            dma((FAR,)),
            dma((NEAR,)),
            dma((NEAR,)),
            pltpu.SemaphoreType.REGULAR((2,)),
        ],
        compiler_params=pltpu.CompilerParams(
            collective_id=0, has_side_effects=True, vmem_limit_bytes=VMEM_BYTES
        ),
    )(
        pltpu.with_memory_space_constraint(brick_position, pltpu.HBM),
        brick_moved,
        pltpu.with_memory_space_constraint(features.reshape(CELLS, WIDTH), pltpu.HBM),
        pltpu.with_memory_space_constraint(cotangent, pltpu.HBM),
        pltpu.with_memory_space_constraint(weight, pltpu.HBM),
    )
    return pl.pallas_call(
        finish,
        out_shape=(
            jax.ShapeDtypeStruct(bricks, BF),
            jax.ShapeDtypeStruct(bricks, BF),
            jax.ShapeDtypeStruct(taps, F32),
        ),
        in_specs=[vmem, vmem, vmem],
        out_specs=(hbm, hbm, hbm),
        scratch_shapes=[
            pltpu.VMEM(taps, F32),
            dma((3,)),
        ],
        compiler_params=pltpu.CompilerParams(vmem_limit_bytes=8 * 1024 * 1024),
    )(conv, grad, summed)


def solution(mesh):
    placed = (
        P(("gx", "gy"), None, None),
        P(("gx", "gy")),
        P(("gx", "gy")),
        P(("gx", "gy")),
        P(),
        P(("gx", "gy"), None, None),
    )
    return jax.shard_map(
        local,
        mesh=mesh,
        in_specs=placed,
        out_specs=(P(("gx", "gy"), None, None), P(("gx", "gy"), None, None), P()),
        check_vma=False,
    )
```
